32 devices in a mesh: groups: 2 (over y), band: 4 (over z), mesh: 2 (over x), feat: 2 (over core).
Axes of the slice: x: 2, y: 2, z: 4, core: 2. Of those that a mesh axis runs over, the one named last changes fastest.
Arguments:
- grid_latent: bfloat16 [16384, 512], P(('groups', 'band', 'mesh')), parts along dimension 0, may hold values from -6 to 6
- mesh_latent: bfloat16 [1024, 512], P(('groups', 'band', 'mesh')), parts along dimension 0, may hold values from -6 to 6
- g2m_send: int32 [24576], P(('groups', 'band', 'mesh')), parts along dimension 0, may hold values from 0 to 1023
- g2m_slot: int32 [24576], P(('groups', 'band', 'mesh')), parts along dimension 0, may hold values from 0 to 1535, as said below
- g2m_recv: int32 [24576], P(('groups', 'band', 'mesh')), parts along dimension 0, may hold values from -1 to 63, as said below
- enc_send_w: bfloat16 [512, 512], P(None, 'feat'), may hold values from -0.25 to 0.25
- enc_recv_w: bfloat16 [512, 512], P(None, 'feat'), may hold values from -0.25 to 0.25
- enc_bias: float32 [512], P('feat'), may hold values from -3 to 3
- enc_out_w: bfloat16 [512, 512], P('feat'), may hold values from -0.25 to 0.25
- enc_gain: float32 [512], replicated, may hold values from 0.1 to 1.9
- proc_send: int32 [8192], P(('groups', 'band', 'mesh')), parts along dimension 0, may hold values from 0 to 63
- proc_slot: int32 [8192], P(('groups', 'band', 'mesh')), parts along dimension 0, may hold values from 0 to 511, as said below
- proc_recv: int32 [8192], P(('groups', 'band', 'mesh')), parts along dimension 0, may hold values from -1 to 63, as said below
- proc_send_w: bfloat16 [512, 512], P(None, 'feat'), may hold values from -0.25 to 0.25
- proc_recv_w: bfloat16 [512, 512], P(None, 'feat'), may hold values from -0.25 to 0.25
- proc_bias: float32 [512], P('feat'), may hold values from -3 to 3
- proc_out_w: bfloat16 [512, 512], P('feat'), may hold values from -0.25 to 0.25
- proc_gain: float32 [512], replicated, may hold values from 0.1 to 1.9
- m2g_send: int32 [49152], P(('groups', 'band', 'mesh', 'feat')), parts along dimension 0, may hold values from 0 to 63
- m2g_slot: int32 [49152], P(('groups', 'band', 'mesh', 'feat')), parts along dimension 0, may hold values from 0 to 1535, as said below
- dec_send_w: bfloat16 [512, 512], replicated, may hold values from -0.25 to 0.25
- dec_recv_w: bfloat16 [512, 512], replicated, may hold values from -0.25 to 0.25
- dec_bias: float32 [512], replicated, may hold values from -3 to 3
- dec_out_w: bfloat16 [512, 512], replicated, may hold values from -0.25 to 0.25
- dec_gain: float32 [512], replicated, may hold values from 0.1 to 1.9
Outputs:
- grid_out: bfloat16 [16384, 512], P(('groups', 'band', 'mesh', 'feat')), parts along dimension 0
- mesh_out: bfloat16 [1024, 512], P(('groups', 'band', 'mesh')), parts along dimension 0
The draws below stay inside these ranges and needn't reach their ends.
There are 2 independent parts, one for each index of `groups`. The reference program is written for one: setup_inputs(seed, part) draws one part's arguments, and reference() takes and returns one part's arrays. A program takes and returns all parts, laid end to end along the dimension named above; an argument that names none is the same for every part. Nothing has to cross between parts.
Inputs may be any that keep to these rules, and one draw needn't show every extreme that they name: `g2m_slot`: entry e of shard q names slot (d * 2 + j) * 256 + s: the s-th row that the shard of mesh index j in band (band of q) + d - 1 sends to shard q; that band exists for every live edge. Padding edges hold 0. `g2m_recv`: live edges come first, in ascending order of receiver; every shard has at least one padding edge. `proc_slot`: entry e of shard q names slot p * 64 + s: the s-th row shard p sends to shard q. Padding edges hold 0. `proc_recv`: live edges come first, in ascending order of receiver; every shard has at least one padding edge. `m2g_slot`: entry 3 g + k names slot (d * 2 + j) * 256 + s of the rows sent for grid node g's decoding device by the shard of mesh index j in band (band of g) + d - 1; that band exists.
All inputs are finite; a program needn't handle non-finite values.
Results may differ from the reference program's by a relative error of at most 0.013.
Values may be sent and summed in bfloat16 or wider, within the bound.
A program may use at most 64 MiB of HBM per device.

```python
import jax
import jax.numpy as jnp
from jax import lax

D = 512
GN_DEV = 1024
MN_DEV = 64
SHARDS = 8
GHALF = 512
GRID = 8192
MESH = 512
ENC_EDGES = 1536
PROC_EDGES = 512
CAP_G = 256
CAP_H = 64
CAP_M = 256
N_BAND = 4
N_MESH = 2
N_FEAT = 2


def slot_block(key, count, total, valid, offset):
    first, second = jax.random.split(key)
    order = jax.random.permutation(first, total).astype(jnp.int32)
    order = jnp.where(order == total - 1, order[0], order)
    order = order.at[0].set(total - 1)
    extra = jax.random.randint(second, (count,), 0, total).astype(jnp.int32)
    filled = jnp.concatenate([order, jnp.zeros((count - total,), jnp.int32)])
    places = jnp.arange(count, dtype=jnp.int32)
    raw = jnp.where(places < total, filled, extra)
    return (offset + raw % valid).astype(jnp.int32)


def band_range(shard, cap):
    block = N_MESH * cap
    band = shard // N_MESH
    bottom = (band == 0).astype(jnp.int32)
    top = (band == N_BAND - 1).astype(jnp.int32)
    return (3 * block - block * bottom - block * top, block * bottom)


def edge_block(key, shard, count, cap, rows, nearby):
    first, second, third = jax.random.split(key, 3)
    if nearby:
        valid, offset = band_range(shard, cap)
        total = 3 * N_MESH * cap
    else:
        total = SHARDS * cap
        valid, offset = (total, 0)
    slot = slot_block(first, count, total, valid, offset)
    live = count - jax.random.randint(second, (), 1, 65)
    recv = jnp.sort(jax.random.randint(third, (count,), 0, rows).astype(jnp.int32))
    places = jnp.arange(count, dtype=jnp.int32)
    recv = jnp.where(places == live - 1, rows - 1, recv)
    recv = jnp.where(places < live, recv, -1).astype(jnp.int32)
    slot = jnp.where(places < live, slot, 0).astype(jnp.int32)
    return (slot, recv)


def edge_lists(key, salt, count, cap, rows, nearby):
    keys = jax.random.split(jax.random.fold_in(key, salt), SHARDS)
    shards = jnp.arange(SHARDS, dtype=jnp.int32)
    slot, recv = jax.vmap(lambda single, shard: edge_block(single, shard, count, cap, rows, nearby))(keys, shards)
    return (slot.reshape(-1), recv.reshape(-1))


def draw_g2m_slot(key, part):
    return edge_lists(key, 21, ENC_EDGES, CAP_G, MN_DEV, True)[0]


def draw_g2m_recv(key, part):
    return edge_lists(key, 21, ENC_EDGES, CAP_G, MN_DEV, True)[1]


def draw_proc_slot(key, part):
    return edge_lists(key, 22, PROC_EDGES, CAP_H, MN_DEV, False)[0]


def draw_proc_recv(key, part):
    return edge_lists(key, 22, PROC_EDGES, CAP_H, MN_DEV, False)[1]


def draw_m2g_slot(key, part):
    key = jax.random.fold_in(key, 23)
    keys = jax.random.split(key, SHARDS * N_FEAT)
    shards = jnp.arange(SHARDS * N_FEAT, dtype=jnp.int32) // N_FEAT

    def one(single, shard):
        valid, offset = band_range(shard, CAP_M)
        return slot_block(single, 3 * GHALF, 3 * N_MESH * CAP_M, valid, offset)
    slots = jax.vmap(one)(keys, shards)
    return slots.reshape(-1)


def place_ends(entries, key, smallest, top_value):
    longest = entries.shape.index(max(entries.shape))
    spots = []
    for shift in (0, 1):
        where = [jax.random.randint(jax.random.fold_in(key, axis), (), 0, length) for axis, length in enumerate(entries.shape)]
        where[longest] = (where[longest] + shift) % entries.shape[longest]
        spots.append(tuple(where))
    return entries.at[spots[0]].set(smallest).at[spots[1]].set(top_value)


def levels(own_key, extent, cuts, least, largest):
    def one(dim, blocks):
        draws = jax.random.uniform(jax.random.fold_in(jax.random.fold_in(own_key, 6), dim), (blocks,), jnp.float32, least / len(cuts), largest / len(cuts))
        return jnp.repeat(jnp.exp(draws), extent[dim] // blocks).reshape((-1,) + (1,) * (len(extent) - dim - 1))

    level = one(*cuts[0])
    for cut in cuts[1:]:
        level = level * one(*cut)
    return level


def scatter_about(stream_key, dims, scale, bound, pieces=(), kind=jnp.bfloat16):
    entries = scale * jax.random.normal(stream_key, dims, jnp.float32)
    if pieces:
        entries = entries * levels(stream_key, dims, pieces, -0.22, 0.18)
    return jnp.clip(entries, -bound, bound).astype(kind)


def setup_inputs(seed: int = 0, part: int = 0) -> dict:
    streams_of = jax.random.split(jax.random.key(seed), 26)
    part_keys = jax.random.split(jax.random.fold_in(streams_of[25], part), 26)
    grid_latent = scatter_about(part_keys[0], (GRID, D), 1.0, 6.0, ((0, 8),))
    mesh_latent = scatter_about(part_keys[1], (MESH, D), 1.0, 6.0, ((0, 8),))
    g2m_send = place_ends(jax.random.randint(part_keys[2], (SHARDS * 3 * N_MESH * CAP_G,), 0, GN_DEV), jax.random.fold_in(part_keys[2], 1), 0, GN_DEV - 1).astype(jnp.int32)
    g2m_slot = draw_g2m_slot(jax.random.fold_in(jax.random.fold_in(streams_of[25], part), 71), part)
    g2m_recv = draw_g2m_recv(jax.random.fold_in(jax.random.fold_in(streams_of[25], part), 71), part)
    enc_send_w = scatter_about(streams_of[5], (D, D), D ** -0.5, 0.25, ((1, 2),))
    enc_recv_w = scatter_about(streams_of[6], (D, D), D ** -0.5, 0.25, ((1, 2),))
    enc_bias = scatter_about(streams_of[7], (D,), 0.5, 3.0, ((0, 2),), jnp.float32)
    enc_out_w = scatter_about(streams_of[8], (D, D), D ** -0.5, 0.25, ((0, 2),))
    enc_gain = jnp.clip(1.0 + 0.18 * jax.random.normal(streams_of[9], (D,), jnp.float32), 0.1, 1.9)
    proc_send = place_ends(jax.random.randint(part_keys[10], (SHARDS * SHARDS * CAP_H,), 0, MN_DEV), jax.random.fold_in(part_keys[10], 1), 0, MN_DEV - 1).astype(jnp.int32)
    proc_slot = draw_proc_slot(jax.random.fold_in(jax.random.fold_in(streams_of[25], part), 71), part)
    proc_recv = draw_proc_recv(jax.random.fold_in(jax.random.fold_in(streams_of[25], part), 71), part)
    proc_send_w = scatter_about(streams_of[13], (D, D), D ** -0.5, 0.25, ((1, 2),))
    proc_recv_w = scatter_about(streams_of[14], (D, D), D ** -0.5, 0.25, ((1, 2),))
    proc_bias = scatter_about(streams_of[15], (D,), 0.5, 3.0, ((0, 2),), jnp.float32)
    proc_out_w = scatter_about(streams_of[16], (D, D), D ** -0.5, 0.25, ((0, 2),))
    proc_gain = jnp.clip(1.0 + 0.18 * jax.random.normal(streams_of[17], (D,), jnp.float32), 0.1, 1.9)
    m2g_send = place_ends(jax.random.randint(part_keys[18], (SHARDS * N_FEAT * 3 * N_MESH * CAP_M,), 0, MN_DEV), jax.random.fold_in(part_keys[18], 1), 0, MN_DEV - 1).astype(jnp.int32)
    m2g_slot = draw_m2g_slot(jax.random.fold_in(jax.random.fold_in(streams_of[25], part), 71), part)
    dec_send_w = scatter_about(streams_of[20], (D, D), D ** -0.5, 0.25)
    dec_recv_w = scatter_about(streams_of[21], (D, D), D ** -0.5, 0.25)
    dec_bias = scatter_about(streams_of[22], (D,), 0.5, 3.0, (), jnp.float32)
    dec_out_w = scatter_about(streams_of[23], (D, D), D ** -0.5, 0.25)
    dec_gain = jnp.clip(1.0 + 0.18 * jax.random.normal(streams_of[24], (D,), jnp.float32), 0.1, 1.9)
    return {"grid_latent": grid_latent, "mesh_latent": mesh_latent, "g2m_send": g2m_send, "g2m_slot": g2m_slot, "g2m_recv": g2m_recv, "enc_send_w": enc_send_w, "enc_recv_w": enc_recv_w, "enc_bias": enc_bias, "enc_out_w": enc_out_w, "enc_gain": enc_gain, "proc_send": proc_send, "proc_slot": proc_slot, "proc_recv": proc_recv, "proc_send_w": proc_send_w, "proc_recv_w": proc_recv_w, "proc_bias": proc_bias, "proc_out_w": proc_out_w, "proc_gain": proc_gain, "m2g_send": m2g_send, "m2g_slot": m2g_slot, "dec_send_w": dec_send_w, "dec_recv_w": dec_recv_w, "dec_bias": dec_bias, "dec_out_w": dec_out_w, "dec_gain": dec_gain}


def layer_norm(values, gain):
    mean = lax.optimization_barrier(jnp.mean(values, axis=-1, keepdims=True))
    centred = values - mean
    spread = lax.optimization_barrier(jnp.mean(centred * centred, axis=-1, keepdims=True))
    return centred * lax.rsqrt(spread + 1e-05) * gain

def neighbour_sender(table, shard, slot, cap, rows, half):
    block = N_MESH * cap
    side = slot // block
    column = slot // cap % N_MESH
    place = slot % cap
    anchor = jnp.clip((shard // N_MESH + side - 1) * N_MESH + column, 0, SHARDS - 1).astype(jnp.int32)
    return anchor * rows + table[anchor, half, side, shard % N_MESH, place]

def global_sender(table, shard, slot, cap, rows):
    anchor = slot // cap
    place = slot % cap
    return anchor * rows + table[anchor, shard, place]

def patch_section(node_latent, source, locate, slots, receivers, edges, send_w, recv_w, bias, out_w, gain):
    source_proj = jnp.dot(source, send_w, preferred_element_type=jnp.float32).astype(jnp.bfloat16)
    recv_term = jnp.dot(node_latent, recv_w, preferred_element_type=jnp.float32) + bias
    slot_rows = slots.reshape(SHARDS, edges)
    recv_rows = receivers.reshape(SHARDS, edges)

    def one_shard(packed):
        shard, slot, recv = packed
        sender = locate(shard, slot)
        live = recv >= 0
        local = jnp.maximum(recv, 0).astype(jnp.int32)
        own_terms = lax.dynamic_slice_in_dim(recv_term, (shard * MN_DEV).astype(jnp.int32), MN_DEV, 0)
        pre = source_proj[sender].astype(jnp.float32) + own_terms[local]
        hidden = lax.optimization_barrier(jax.nn.silu(pre).astype(jnp.bfloat16)).astype(jnp.float32)
        hidden = jnp.where(live[:, None], hidden, jnp.float32(0.0))
        return jax.ops.segment_sum(hidden, local, num_segments=MN_DEV)
    summed = lax.map(one_shard, (jnp.arange(SHARDS, dtype=jnp.int32), slot_rows, recv_rows))
    summed = summed.reshape(SHARDS * MN_DEV, -1).astype(jnp.bfloat16)
    total = jnp.dot(summed, out_w, preferred_element_type=jnp.float32)
    return (node_latent.astype(jnp.float32) + layer_norm(total, gain)).astype(jnp.bfloat16)

def reference(grid_latent, mesh_latent, g2m_send, g2m_slot, g2m_recv, enc_send_w, enc_recv_w, enc_bias, enc_out_w, enc_gain, proc_send, proc_slot, proc_recv, proc_send_w, proc_recv_w, proc_bias, proc_out_w, proc_gain, m2g_send, m2g_slot, dec_send_w, dec_recv_w, dec_bias, dec_out_w, dec_gain):
    enc_table = g2m_send.reshape(SHARDS, 1, 3, N_MESH, CAP_G)
    proc_table = proc_send.reshape(SHARDS, SHARDS, CAP_H)

    def enc_locate(shard, slot):
        return neighbour_sender(enc_table, shard, slot, CAP_G, GN_DEV, 0)

    def proc_locate(shard, slot):
        return global_sender(proc_table, shard, slot, CAP_H, MN_DEV)
    mesh_first = patch_section(mesh_latent, grid_latent, enc_locate, g2m_slot, g2m_recv, ENC_EDGES, enc_send_w, enc_recv_w, enc_bias, enc_out_w, enc_gain)
    mesh_out = patch_section(mesh_first, mesh_first, proc_locate, proc_slot, proc_recv, PROC_EDGES, proc_send_w, proc_recv_w, proc_bias, proc_out_w, proc_gain)
    dec_proj = jnp.dot(mesh_out, dec_send_w, preferred_element_type=jnp.float32).astype(jnp.bfloat16)
    dec_table = m2g_send.reshape(SHARDS, N_FEAT, 3, N_MESH, CAP_M)
    slot_rows = m2g_slot.reshape(SHARDS * N_FEAT, 3 * GHALF)
    grid_rows = grid_latent.reshape(SHARDS * N_FEAT, GHALF, -1)
    blocks = jnp.arange(SHARDS * N_FEAT, dtype=jnp.int32)

    def one_block(packed):
        block, slot, own = packed
        shard = block // N_FEAT
        half = block % N_FEAT
        sender = neighbour_sender(dec_table, shard, slot, CAP_M, MN_DEV, half)
        recv_term = jnp.dot(own, dec_recv_w, preferred_element_type=jnp.float32) + dec_bias
        pre = dec_proj[sender].astype(jnp.float32).reshape(GHALF, 3, -1) + recv_term[:, None, :]
        hidden = jax.nn.silu(pre).astype(jnp.bfloat16)
        summed = lax.optimization_barrier(jnp.sum(hidden, axis=1, dtype=jnp.float32)).astype(jnp.bfloat16)
        total = jnp.dot(summed, dec_out_w, preferred_element_type=jnp.float32)
        return (own.astype(jnp.float32) + layer_norm(total, dec_gain)).astype(jnp.bfloat16)
    grid_out = lax.map(one_block, (blocks, slot_rows, grid_rows)).reshape(SHARDS * GN_DEV, -1)
    return (grid_out, mesh_out)
```

```python
import functools

import jax
import jax.numpy as jnp
from jax import lax
from jax.experimental import pallas as pl
from jax.experimental.pallas import tpu as pltpu
from jax.sharding import PartitionSpec as P

MESH = pl.DeviceIdType.MESH
LANES = 128
BF = jnp.bfloat16
F32 = jnp.float32


def dot(a, b):
    return jnp.dot(a, b, preferred_element_type=F32)


def normed(values, gain):
    mean = jnp.mean(values, axis=-1, keepdims=True)
    centred = values - mean
    spread = jnp.mean(centred * centred, axis=-1, keepdims=True)
    return centred * lax.rsqrt(spread + 1e-05) * gain


def silu(x):
    half = 0.5 * x
    return half + half * jnp.tanh(half)


def columns(row):
    return jnp.transpose(jnp.broadcast_to(row, (LANES, row.shape[1])))


def pick(cols, width):
    lane = lax.broadcasted_iota(jnp.int32, cols.shape, 1)
    if width < LANES:
        cols, lane = cols[:, :width], lane[:, :width]
        return jnp.where(cols == lane, 1.0, 0.0).astype(BF)
    parts = [
        jnp.where(cols == lane + t * LANES, 1.0, 0.0).astype(BF) for t in range(width // LANES)
    ]
    return parts[0] if len(parts) == 1 else jnp.concatenate(parts, axis=1)


def kernel(
    nb, nm, cap_g, cap_h, cap_m,
    grid_ref, mesh_ref, g_send, g_slot, g_recv, e_sw, e_rw, e_b, e_ow, e_g,
    p_send, p_slot, p_recv, p_sw, p_rw, p_b, p_ow, p_g,
    m_send, m_slot, d_sw, d_rw, d_b, d_ow, d_g,
    grid_out, mesh_out,
    gp, ebuf, erecv, ecol, hid, hid2, own_term, pbuf, precv, iref, dcol, dproj, dtab,
    part, other,
    es, er, is_, ir, ps, pr, ds, dr, fs, fr,
):
    shards = nb * nm
    band, col, feat = lax.axis_index("band"), lax.axis_index("mesh"), lax.axis_index("feat")
    me = band * nm + col
    mrows = mesh_ref.shape[0]
    half = grid_out.shape[0]
    dh = e_sw.shape[1]
    near = 3 * nm

    def at_shard(shard):
        return {"band": shard // nm, "mesh": lax.rem(shard, nm)}

    barrier = pltpu.get_barrier_semaphore()
    for o in range(1, shards):
        peer = lax.rem(me + o, shards)
        pl.semaphore_signal(barrier, inc=1, device_id=at_shard(peer), device_id_type=MESH)
    pl.semaphore_signal(barrier, inc=1, device_id={"feat": 1 - feat}, device_id_type=MESH)

    gp[...] = dot(grid_ref[...], e_sw[...]).astype(BF)
    for d, edge in ((0, 0), (2, nb - 1)):
        @pl.when(band == edge)
        def _(d=d):
            for j in range(nm):
                i = d * nm + j
                erecv[i] = jnp.zeros(erecv.shape[1:], BF)
                iref[i] = jnp.zeros(iref.shape[1:], jnp.int32)
                dtab[i] = jnp.zeros(dtab.shape[1:], BF)

    pl.semaphore_wait(barrier, shards)

    def near_copy(src, dst, send, recv, d, o):
        to = lax.rem(col + o, nm)
        return pltpu.make_async_remote_copy(
            src_ref=src(d * nm + to),
            dst_ref=dst.at[d * nm + col],
            send_sem=send.at[d * nm + o],
            recv_sem=recv.at[d * nm + col],
            device_id={"band": band + 1 - d, "mesh": to},
            device_id_type=MESH,
        )

    def near_arrival(dst, send, recv, d, o):
        source = lax.rem(col + o, nm)
        return pltpu.make_async_remote_copy(
            src_ref=dst.at[d * nm + source],
            dst_ref=dst.at[d * nm + source],
            send_sem=send.at[d * nm + o],
            recv_sem=recv.at[d * nm + source],
            device_id={"band": band + d - 1, "mesh": source},
            device_id_type=MESH,
        )

    def to_there(d):
        return {0: band + 1 < nb, 2: band > 0, 1: None}[d]

    def from_there(d):
        return {0: band > 0, 2: band + 1 < nb, 1: None}[d]

    def when(cond, f):
        if cond is None:
            f()
        else:
            pl.when(cond)(f)

    order = [(d, o) for d in (0, 2, 1) for o in reversed(range(nm)) if (d, o) != (1, 0)]

    for d, o in order:
        when(to_there(d), lambda d=d, o=o: near_copy(lambda i: m_send.at[i], iref, is_, ir, d, o).start())
    iref[nm + col] = m_send[nm + col]

    def gathered(i):
        return dot(pick(columns(g_send[i]), gp.shape[0]), gp[...]).astype(BF)

    for d, o in order:
        def send(d=d, o=o):
            i = d * nm + lax.rem(col + o, nm)
            ebuf[i] = gathered(i)
            near_copy(lambda i: ebuf.at[i], erecv, es, er, d, o).start()
        when(to_there(d), send)
    erecv[nm + col] = gathered(nm + col)

    own = pl.ds(pl.multiple_of(feat * half, half), half)
    own_term[...] = dot(grid_ref[own, :], d_rw[...]) + d_b[...]

    def split_term(values, weight, bias):
        term = dot(values, weight[...]) + bias[...]
        high = term.astype(BF)
        return jnp.concatenate([high, (term - high.astype(F32)).astype(BF)], axis=0)

    def pick2(cols):
        lane = lax.broadcasted_iota(jnp.int32, cols.shape, 1)
        if 2 * mrows == LANES:
            lane = jnp.where(lane >= mrows, lane - mrows, lane)
            return jnp.where(cols == lane, 1.0, 0.0).astype(BF)
        single = pick(cols, mrows)
        return jnp.concatenate([single, single], axis=1)

    eterm = split_term(mesh_ref[...], e_rw, e_b)

    for d, o in order:
        when(from_there(d), lambda d=d, o=o: near_arrival(iref, is_, ir, d, o).wait_recv())
    nedge = m_slot.shape[0] * m_slot.shape[2]
    tables = [columns(iref[i]).astype(F32).astype(BF) for i in range(near)]
    for k in range(3):
        slots = columns(m_slot[k])
        block = jnp.zeros(slots.shape, jnp.int32)
        row = jnp.zeros(slots.shape, F32)
        for i in range(near):
            row = row + dot(pick(slots - i * cap_m, cap_m), tables[i])
            if i:
                block = block + jnp.where(slots >= i * cap_m, mrows, 0)
        dcol[pl.ds(k * half, half), :] = block + (row + 0.5).astype(jnp.int32)

    ecol[0] = columns(g_slot[...])
    ecol[1] = columns(g_recv[...])
    for d, o in order:
        when(from_there(d), lambda d=d, o=o: near_arrival(erecv, es, er, d, o).wait_recv())
    chunk = 256

    def edges(c, carry):
        rows = pl.ds(pl.multiple_of(c * chunk, chunk), chunk)
        pre = dot(pick(ecol[0, rows, :], near * cap_g), erecv[...].reshape(near * cap_g, dh))
        pre = pre.astype(BF).astype(F32) + dot(pick2(ecol[1, rows, :]), eterm)
        hid[rows, :] = silu(pre).astype(BF)
        return carry

    lax.fori_loop(0, hid.shape[0] // chunk, edges, 0)

    def finish(base, recv, hidden, ow, gain, n):
        place = lax.broadcasted_iota(jnp.int32, (mrows, recv.shape[1]), 0)
        onto = jnp.where(recv[...] == place, 1.0, 0.0).astype(BF)
        summed = dot(onto, hidden[...]).astype(BF)
        part[n] = dot(summed, ow[...]).astype(BF)
        copy = pltpu.make_async_remote_copy(
            src_ref=part.at[n], dst_ref=other.at[n], send_sem=fs.at[n], recv_sem=fr.at[n],
            device_id={"feat": 1 - feat}, device_id_type=MESH,
        )
        copy.start()
        copy.wait()
        total = part[n].astype(F32) + other[n].astype(F32)
        return (base.astype(F32) + normed(total, gain[...])).astype(BF)

    psend_pick = pick(columns(p_send[...]), mrows)
    pslot_pick = pick(columns(p_slot[...]), shards * cap_h)
    precv_pick = pick2(columns(p_recv[...]))
    first = finish(mesh_ref[...], g_recv, hid, e_ow, e_g, 0)

    mproj = dot(first, p_sw[...]).astype(BF)
    pbuf[...] = dot(psend_pick, mproj).astype(BF).reshape(pbuf.shape)

    def proc_copy(o):
        peer = lax.rem(me + o, shards)
        return pltpu.make_async_remote_copy(
            src_ref=pbuf.at[peer], dst_ref=precv.at[me], send_sem=ps.at[o], recv_sem=pr.at[me],
            device_id=at_shard(peer), device_id_type=MESH,
        )

    def proc_arrival(o):
        peer = lax.rem(me + o, shards)
        return pltpu.make_async_remote_copy(
            src_ref=precv.at[peer], dst_ref=precv.at[peer], send_sem=ps.at[o],
            recv_sem=pr.at[peer], device_id=at_shard(peer), device_id_type=MESH,
        )

    for o in range(1, shards):
        proc_copy(o).start()
    precv[me] = pbuf[me]
    pterm = dot(precv_pick, split_term(first, p_rw, p_b))
    for o in range(1, shards):
        proc_arrival(o).wait_recv()
    pre = dot(pslot_pick, precv[...].reshape(shards * cap_h, dh)) + pterm
    hid2[...] = silu(pre).astype(BF)
    last = finish(first, p_recv, hid2, p_ow, p_g, 1)
    mesh_out[...] = last

    projected = dot(last, d_sw[...]).astype(BF)
    dproj[...] = projected
    for d, o in order:
        when(to_there(d), lambda d=d, o=o: near_copy(lambda i: dproj, dtab, ds, dr, d, o).start())
    dtab[nm + col] = projected
    for d, o in order:
        when(from_there(d), lambda d=d, o=o: near_arrival(dtab, ds, dr, d, o).wait_recv())
    dchunk = 128

    def decode(c, carry):
        rows = pl.ds(pl.multiple_of(c * dchunk, dchunk), dchunk)
        term = own_term[rows, :]
        table = dtab[...].reshape(near * mrows, dtab.shape[2])
        summed = jnp.zeros(term.shape, F32)
        for k in range(3):
            idx = dcol[pl.ds(pl.multiple_of(k * half + c * dchunk, dchunk), dchunk), :]
            pre = dot(pick(idx, near * mrows), table) + term
            summed = summed + silu(pre).astype(BF).astype(F32)
        decoded = dot(summed.astype(BF), d_ow[...])
        base = grid_ref[pl.ds(pl.multiple_of(feat * half + c * dchunk, dchunk), dchunk), :]
        grid_out[rows, :] = (base.astype(F32) + normed(decoded, d_g[...])).astype(BF)
        return carry

    lax.fori_loop(0, half // dchunk, decode, 0)

    for d, o in order:
        def done(d=d, o=o):
            near_copy(lambda i: m_send.at[i], iref, is_, ir, d, o).wait_send()
            near_copy(lambda i: ebuf.at[i], erecv, es, er, d, o).wait_send()
            near_copy(lambda i: dproj, dtab, ds, dr, d, o).wait_send()
        when(to_there(d), done)
    for o in range(1, shards):
        proc_copy(o).wait_send()


def per_device(
    grid_latent, mesh_latent,
    g2m_send, g2m_slot, g2m_recv, enc_send_w, enc_recv_w, enc_bias, enc_out_w, enc_gain,
    proc_send, proc_slot, proc_recv, proc_send_w, proc_recv_w, proc_bias, proc_out_w, proc_gain,
    m2g_send, m2g_slot, dec_send_w, dec_recv_w, dec_bias, dec_out_w, dec_gain,
):
    nb, nm = lax.axis_size("band"), lax.axis_size("mesh")
    shards, near = nb * nm, 3 * nm
    rows, width = grid_latent.shape
    mrows = mesh_latent.shape[0]
    half = rows // lax.axis_size("feat")
    dh = enc_send_w.shape[1]
    cap_g = g2m_send.shape[0] // near
    cap_m = m2g_send.shape[0] // near
    cap_h = proc_send.shape[0] // shards
    if cap_h % 16:
        padded = -(-cap_h // 16) * 16
        proc_send = jnp.pad(proc_send.reshape(shards, cap_h), ((0, 0), (0, padded - cap_h)))
        proc_slot = proc_slot // cap_h * padded + proc_slot % cap_h
        cap_h = padded
    row = lambda v: v.reshape(1, -1)
    args = (
        grid_latent, mesh_latent,
        g2m_send.reshape(near, 1, cap_g), row(g2m_slot), row(g2m_recv),
        enc_send_w, enc_recv_w, row(enc_bias), enc_out_w, row(enc_gain),
        row(proc_send), row(proc_slot), row(proc_recv),
        proc_send_w, proc_recv_w, row(proc_bias), proc_out_w, row(proc_gain),
        m2g_send.reshape(near, 1, cap_m), m2g_slot.reshape(half, 3).T.reshape(3, 1, half),
        dec_send_w, dec_recv_w, row(dec_bias), dec_out_w, row(dec_gain),
    )
    vmem = pl.BlockSpec(memory_space=pltpu.VMEM)
    dma = pltpu.SemaphoreType.DMA
    scratch = [
        pltpu.VMEM((rows, dh), BF),
        pltpu.VMEM((near, cap_g, dh), BF),
        pltpu.VMEM((near, cap_g, dh), BF),
        pltpu.VMEM((2, g2m_slot.shape[0], LANES), jnp.int32),
        pltpu.VMEM((g2m_slot.shape[0], dh), BF),
        pltpu.VMEM((proc_slot.shape[0], dh), BF),
        pltpu.VMEM((half, width), F32),
        pltpu.VMEM((shards, cap_h, dh), BF),
        pltpu.VMEM((shards, cap_h, dh), BF),
        pltpu.VMEM((near, 1, cap_m), jnp.int32),
        pltpu.VMEM((3 * half, LANES), jnp.int32),
        pltpu.VMEM((mrows, width), BF),
        pltpu.VMEM((near, mrows, width), BF),
        pltpu.VMEM((2, mrows, width), BF),
        pltpu.VMEM((2, mrows, width), BF),
        dma((near,)), dma((near,)), dma((near,)), dma((near,)),
        dma((shards,)), dma((shards,)), dma((near,)), dma((near,)),
        dma((2,)), dma((2,)),
    ]
    grid_out, mesh_out = pl.pallas_call(
        functools.partial(kernel, nb, nm, cap_g, cap_h, cap_m),
        out_shape=(
            jax.ShapeDtypeStruct((half, width), BF),
            jax.ShapeDtypeStruct((mrows, width), BF),
        ),
        in_specs=[vmem] * len(args),
        out_specs=(vmem, vmem),
        scratch_shapes=scratch,
        compiler_params=pltpu.CompilerParams(
            collective_id=0, has_side_effects=True, vmem_limit_bytes=48 * 1024 * 1024
        ),
    )(*args)
    return (grid_out, mesh_out)


def solution(mesh):
    shard = P(("groups", "band", "mesh"))
    rows = P(("groups", "band", "mesh"), None)
    finer = P(("groups", "band", "mesh", "feat"))
    layer = (P(None, "feat"), P(None, "feat"), P("feat"), P("feat", None), P())
    return jax.shard_map(
        per_device,
        mesh=mesh,
        in_specs=(rows, rows, shard, shard, shard, *layer, shard, shard, shard, *layer,
                  finer, finer, P(), P(), P(), P(), P()),
        out_specs=(P(("groups", "band", "mesh", "feat"), None), rows),
        check_vma=False,
    )
```

```python
import functools

import jax
import jax.numpy as jnp
from jax import lax
from jax.experimental import pallas as pl
from jax.experimental.pallas import tpu as pltpu
from jax.sharding import PartitionSpec as P

MESH = pl.DeviceIdType.MESH
LANES = 128
BF = jnp.bfloat16
F32 = jnp.float32


def dot(a, b):
    return jnp.dot(a, b, preferred_element_type=F32)


def normed(values, gain):
    mean = jnp.mean(values, axis=-1, keepdims=True)
    centred = values - mean
    spread = jnp.mean(centred * centred, axis=-1, keepdims=True)
    return centred * lax.rsqrt(spread + 1e-05) * gain


def silu(x):
    half = 0.5 * x
    return half + half * jnp.tanh(half)


def columns(row):
    return jnp.transpose(jnp.broadcast_to(row, (LANES, row.shape[1])))


def pick(cols, width):
    lane = lax.broadcasted_iota(jnp.int32, cols.shape, 1)
    if width < LANES:
        cols, lane = cols[:, :width], lane[:, :width]
        return jnp.where(cols == lane, 1.0, 0.0).astype(BF)
    parts = [
        jnp.where(cols == lane + t * LANES, 1.0, 0.0).astype(BF) for t in range(width // LANES)
    ]
    return parts[0] if len(parts) == 1 else jnp.concatenate(parts, axis=1)


NAMES = (
    "grid", "mesh", "g_send", "g_slot", "g_recv", "e_sw", "e_rw", "e_b", "e_ow", "e_g",
    "p_send", "p_slot", "p_recv", "p_sw", "p_rw", "p_b", "p_ow", "p_g",
    "m_send", "m_slot", "d_sw", "d_rw", "d_b", "d_ow", "d_g",
)
FIRST = ("g_send", "e_sw", "grid", "m_send")
SECOND = ("d_rw", "d_b", "mesh", "e_rw", "e_b", "m_slot", "g_slot", "g_recv", "e_ow", "e_g")
THIRD = ("p_send", "p_slot", "p_recv", "p_sw", "p_rw", "p_b", "p_ow", "p_g", "d_sw", "d_ow", "d_g")


def kernel(nb, nm, cap_g, cap_h, cap_m, *refs):
    count = len(NAMES)
    sources = dict(zip(NAMES, refs[:count]))
    grid_out, mesh_out = refs[count : count + 2]
    here = dict(zip(NAMES, refs[count + 2 : 2 * count + 2]))
    (
        gp, ebuf, erecv, ecol, hid, hid2, gcol, own_term, pbuf, precv, mbuf, iref, dcol, dproj, dtab,
        part, other, ls,
        es, er, is_, ir, ps, pr, ds, dr, fs, fr,
    ) = refs[2 * count + 2 :]

    def fetch(name):
        return pltpu.make_async_copy(sources[name], here[name], ls.at[NAMES.index(name)])

    def ready(*names):
        for name in names:
            fetch(name).wait()

    for name in FIRST:
        fetch(name).start()

    def flat(name):
        value = here[name][...]
        return value.reshape(1, value.shape[0])

    grid_ref, mesh_ref = here["grid"], here["mesh"]
    e_sw, e_rw, e_ow = here["e_sw"], here["e_rw"], here["e_ow"]
    p_sw, p_rw, p_ow = here["p_sw"], here["p_rw"], here["p_ow"]
    d_sw, d_rw, d_ow = here["d_sw"], here["d_rw"], here["d_ow"]
    band, col, feat = lax.axis_index("band"), lax.axis_index("mesh"), lax.axis_index("feat")
    me = band * nm + col
    shards = nb * nm
    mrows = mesh_ref.shape[0]
    half = grid_out.shape[0]
    dh = e_sw.shape[1]
    near = 3 * nm

    def at_shard(shard):
        return {"band": shard // nm, "mesh": lax.rem(shard, nm)}

    barrier = pltpu.get_barrier_semaphore()
    for o in range(1, shards):
        peer = lax.rem(me + o, shards)
        pl.semaphore_signal(barrier, inc=1, device_id=at_shard(peer), device_id_type=MESH)
    pl.semaphore_signal(barrier, inc=1, device_id={"feat": 1 - feat}, device_id_type=MESH)

    for name in SECOND:
        fetch(name).start()
    ready("g_send", "e_sw", "grid", "m_send")
    gp[...] = dot(grid_ref[...], e_sw[...]).astype(BF)
    for d, edge in ((0, 0), (2, nb - 1)):
        @pl.when(band == edge)
        def _(d=d):
            for j in range(nm):
                i = d * nm + j
                erecv[i] = jnp.zeros(erecv.shape[1:], BF)
                iref[i] = jnp.zeros(iref.shape[1:], jnp.int32)
                dtab[i] = jnp.zeros(dtab.shape[1:], BF)

    pl.semaphore_wait(barrier, shards)

    def near_copy(src, dst, send, recv, d, o):
        to = lax.rem(col + o, nm)
        return pltpu.make_async_remote_copy(
            src_ref=src(d * nm + to),
            dst_ref=dst.at[d * nm + col],
            send_sem=send.at[d * nm + o],
            recv_sem=recv.at[d * nm + col],
            device_id={"band": band + 1 - d, "mesh": to},
            device_id_type=MESH,
        )

    def near_arrival(dst, send, recv, d, o):
        source = lax.rem(col + o, nm)
        return pltpu.make_async_remote_copy(
            src_ref=dst.at[d * nm + source],
            dst_ref=dst.at[d * nm + source],
            send_sem=send.at[d * nm + o],
            recv_sem=recv.at[d * nm + source],
            device_id={"band": band + d - 1, "mesh": source},
            device_id_type=MESH,
        )

    def to_there(d):
        return {0: band + 1 < nb, 2: band > 0, 1: None}[d]

    def from_there(d):
        return {0: band > 0, 2: band + 1 < nb, 1: None}[d]

    def when(cond, f):
        if cond is None:
            f()
        else:
            pl.when(cond)(f)

    order = [(d, o) for d in (0, 2, 1) for o in reversed(range(nm)) if (d, o) != (1, 0)]

    for name in THIRD:
        fetch(name).start()

    for i in range(near):
        mbuf[i] = flat("m_send")[:, i * cap_m : (i + 1) * cap_m]
    for d, o in order:
        when(to_there(d), lambda d=d, o=o: near_copy(lambda i: mbuf.at[i], iref, is_, ir, d, o).start())
    iref[nm + col] = mbuf[nm + col]

    for i in range(near):
        gcol[i] = columns(flat("g_send")[:, i * cap_g : (i + 1) * cap_g])

    def gathered(i):
        return dot(pick(gcol[i], gp.shape[0]), gp[...]).astype(BF)

    for d, o in order:
        def send(d=d, o=o):
            i = d * nm + lax.rem(col + o, nm)
            ebuf[i] = gathered(i)
            near_copy(lambda i: ebuf.at[i], erecv, es, er, d, o).start()
        when(to_there(d), send)
    erecv[nm + col] = gathered(nm + col)

    ready(*SECOND)
    own = pl.ds(pl.multiple_of(feat * half, half), half)
    own_term[...] = dot(grid_ref[own, :], d_rw[...]) + flat("d_b")

    def split_term(values, weight, bias):
        term = dot(values, weight[...]) + bias
        high = term.astype(BF)
        return jnp.concatenate([high, (term - high.astype(F32)).astype(BF)], axis=0)

    def pick2(cols):
        lane = lax.broadcasted_iota(jnp.int32, cols.shape, 1)
        if 2 * mrows == LANES:
            lane = jnp.where(lane >= mrows, lane - mrows, lane)
            return jnp.where(cols == lane, 1.0, 0.0).astype(BF)
        single = pick(cols, mrows)
        return jnp.concatenate([single, single], axis=1)

    eterm = split_term(mesh_ref[...], e_rw, flat("e_b"))

    for d, o in order:
        when(from_there(d), lambda d=d, o=o: near_arrival(iref, is_, ir, d, o).wait_recv())
    tables = [columns(iref[i]).astype(F32).astype(BF) for i in range(near)]
    for k in range(3):
        slots = columns(flat("m_slot")[:, k * half : (k + 1) * half])
        block = jnp.zeros(slots.shape, jnp.int32)
        row = jnp.zeros(slots.shape, F32)
        for i in range(near):
            row = row + dot(pick(slots - i * cap_m, cap_m), tables[i])
            if i:
                block = block + jnp.where(slots >= i * cap_m, mrows, 0)
        dcol[pl.ds(k * half, half), :] = block + (row + 0.5).astype(jnp.int32)

    ecol[0] = columns(flat("g_slot"))
    ecol[1] = columns(flat("g_recv"))
    for d, o in order:
        when(from_there(d), lambda d=d, o=o: near_arrival(erecv, es, er, d, o).wait_recv())
    chunk = 256

    def edges(c, carry):
        rows = pl.ds(pl.multiple_of(c * chunk, chunk), chunk)
        pre = dot(pick(ecol[0, rows, :], near * cap_g), erecv[...].reshape(near * cap_g, dh))
        pre = pre.astype(BF).astype(F32) + dot(pick2(ecol[1, rows, :]), eterm)
        hid[rows, :] = silu(pre).astype(BF)
        return carry

    lax.fori_loop(0, hid.shape[0] // chunk, edges, 0)

    def finish(base, recv, hidden, ow, gain, n):
        place = lax.broadcasted_iota(jnp.int32, (mrows, recv.shape[1]), 0)
        onto = jnp.where(recv == place, 1.0, 0.0).astype(BF)
        summed = dot(onto, hidden[...]).astype(BF)
        part[n] = dot(summed, ow[...]).astype(BF)
        copy = pltpu.make_async_remote_copy(
            src_ref=part.at[n], dst_ref=other.at[n], send_sem=fs.at[n], recv_sem=fr.at[n],
            device_id={"feat": 1 - feat}, device_id_type=MESH,
        )
        copy.start()
        copy.wait()
        total = part[n].astype(F32) + other[n].astype(F32)
        return (base.astype(F32) + normed(total, gain)).astype(BF)

    ready(*THIRD)
    psend_pick = pick(columns(flat("p_send")), mrows)
    pslot_pick = pick(columns(flat("p_slot")), shards * cap_h)
    precv_pick = pick2(columns(flat("p_recv")))
    first = finish(mesh_ref[...], flat("g_recv"), hid, e_ow, flat("e_g"), 0)

    mproj = dot(first, p_sw[...]).astype(BF)
    pbuf[...] = dot(psend_pick, mproj).astype(BF).reshape(pbuf.shape)

    def proc_copy(o):
        peer = lax.rem(me + o, shards)
        return pltpu.make_async_remote_copy(
            src_ref=pbuf.at[peer], dst_ref=precv.at[me], send_sem=ps.at[o], recv_sem=pr.at[me],
            device_id=at_shard(peer), device_id_type=MESH,
        )

    def proc_arrival(o):
        peer = lax.rem(me + o, shards)
        return pltpu.make_async_remote_copy(
            src_ref=precv.at[peer], dst_ref=precv.at[peer], send_sem=ps.at[o],
            recv_sem=pr.at[peer], device_id=at_shard(peer), device_id_type=MESH,
        )

    for o in range(1, shards):
        proc_copy(o).start()
    precv[me] = pbuf[me]
    pterm = dot(precv_pick, split_term(first, p_rw, flat("p_b")))
    for o in range(1, shards):
        proc_arrival(o).wait_recv()
    pre = dot(pslot_pick, precv[...].reshape(shards * cap_h, dh)) + pterm
    hid2[...] = silu(pre).astype(BF)
    last = finish(first, flat("p_recv"), hid2, p_ow, flat("p_g"), 1)
    mesh_out[...] = last

    projected = dot(last, d_sw[...]).astype(BF)
    dproj[...] = projected
    for d, o in order:
        when(to_there(d), lambda d=d, o=o: near_copy(lambda i: dproj, dtab, ds, dr, d, o).start())
    dtab[nm + col] = projected
    for d, o in order:
        when(from_there(d), lambda d=d, o=o: near_arrival(dtab, ds, dr, d, o).wait_recv())
    dchunk = 128

    def decode(c, carry):
        rows = pl.ds(pl.multiple_of(c * dchunk, dchunk), dchunk)
        term = own_term[rows, :]
        table = dtab[...].reshape(near * mrows, dtab.shape[2])
        summed = jnp.zeros(term.shape, F32)
        for k in range(3):
            idx = dcol[pl.ds(3 * c * dchunk + k, dchunk, stride=3), :]
            pre = dot(pick(idx, near * mrows), table) + term
            summed = summed + silu(pre).astype(BF).astype(F32)
        decoded = dot(summed.astype(BF), d_ow[...])
        base = grid_ref[pl.ds(pl.multiple_of(feat * half + c * dchunk, dchunk), dchunk), :]
        grid_out[rows, :] = (base.astype(F32) + normed(decoded, flat("d_g"))).astype(BF)
        return carry

    lax.fori_loop(0, half // dchunk, decode, 0)

    for d, o in order:
        def done(d=d, o=o):
            near_copy(lambda i: mbuf.at[i], iref, is_, ir, d, o).wait_send()
            near_copy(lambda i: ebuf.at[i], erecv, es, er, d, o).wait_send()
            near_copy(lambda i: dproj, dtab, ds, dr, d, o).wait_send()
        when(to_there(d), done)
    for o in range(1, shards):
        proc_copy(o).wait_send()


def per_device(
    grid_latent, mesh_latent,
    g2m_send, g2m_slot, g2m_recv, enc_send_w, enc_recv_w, enc_bias, enc_out_w, enc_gain,
    proc_send, proc_slot, proc_recv, proc_send_w, proc_recv_w, proc_bias, proc_out_w, proc_gain,
    m2g_send, m2g_slot, dec_send_w, dec_recv_w, dec_bias, dec_out_w, dec_gain,
):
    nb, nm = lax.axis_size("band"), lax.axis_size("mesh")
    shards, near = nb * nm, 3 * nm
    rows, width = grid_latent.shape
    mrows = mesh_latent.shape[0]
    half = rows // lax.axis_size("feat")
    dh = enc_send_w.shape[1]
    cap_g = g2m_send.shape[0] // near
    cap_m = m2g_send.shape[0] // near
    cap_h = proc_send.shape[0] // shards
    if cap_h % 16:
        padded = -(-cap_h // 16) * 16
        proc_send = jnp.pad(proc_send.reshape(shards, cap_h), ((0, 0), (0, padded - cap_h))).reshape(-1)
        proc_slot = proc_slot // cap_h * padded + proc_slot % cap_h
        cap_h = padded
    args = (
        grid_latent, mesh_latent,
        g2m_send, g2m_slot, g2m_recv, enc_send_w, enc_recv_w, enc_bias, enc_out_w, enc_gain,
        proc_send, proc_slot, proc_recv,
        proc_send_w, proc_recv_w, proc_bias, proc_out_w, proc_gain,
        m2g_send, m2g_slot, dec_send_w, dec_recv_w, dec_bias, dec_out_w, dec_gain,
    )
    hbm = pl.BlockSpec(memory_space=pltpu.HBM)
    vmem = pl.BlockSpec(memory_space=pltpu.VMEM)
    dma = pltpu.SemaphoreType.DMA
    scratch = [pltpu.VMEM(v.shape, v.dtype) for v in args] + [
        pltpu.VMEM((rows, dh), BF),
        pltpu.VMEM((near, cap_g, dh), BF),
        pltpu.VMEM((near, cap_g, dh), BF),
        pltpu.VMEM((2, g2m_slot.shape[0], LANES), jnp.int32),
        pltpu.VMEM((g2m_slot.shape[0], dh), BF),
        pltpu.VMEM((proc_slot.shape[0], dh), BF),
        pltpu.VMEM((near, cap_g, LANES), jnp.int32),
        pltpu.VMEM((half, width), F32),
        pltpu.VMEM((shards, cap_h, dh), BF),
        pltpu.VMEM((shards, cap_h, dh), BF),
        pltpu.VMEM((near, 1, cap_m), jnp.int32),
        pltpu.VMEM((near, 1, cap_m), jnp.int32),
        pltpu.VMEM((3 * half, LANES), jnp.int32),
        pltpu.VMEM((mrows, width), BF),
        pltpu.VMEM((near, mrows, width), BF),
        pltpu.VMEM((2, mrows, width), BF),
        pltpu.VMEM((2, mrows, width), BF),
        dma((len(args),)),
        dma((near,)), dma((near,)), dma((near,)), dma((near,)),
        dma((shards,)), dma((shards,)), dma((near,)), dma((near,)),
        dma((2,)), dma((2,)),
    ]
    grid_out, mesh_out = pl.pallas_call(
        functools.partial(kernel, nb, nm, cap_g, cap_h, cap_m),
        out_shape=(
            jax.ShapeDtypeStruct((half, width), BF),
            jax.ShapeDtypeStruct((mrows, width), BF),
        ),
        in_specs=[hbm] * len(args),
        out_specs=(vmem, vmem),
        scratch_shapes=scratch,
        compiler_params=pltpu.CompilerParams(
            collective_id=0, has_side_effects=True, vmem_limit_bytes=64 * 1024 * 1024
        ),
    )(*args)
    return (grid_out, mesh_out)


def solution(mesh):
    shard = P(("groups", "band", "mesh"))
    rows = P(("groups", "band", "mesh"), None)
    finer = P(("groups", "band", "mesh", "feat"))
    layer = (P(None, "feat"), P(None, "feat"), P("feat"), P("feat", None), P())
    return jax.shard_map(
        per_device,
        mesh=mesh,
        in_specs=(rows, rows, shard, shard, shard, *layer, shard, shard, shard, *layer,
                  finer, finer, P(), P(), P(), P(), P()),
        out_specs=(P(("groups", "band", "mesh", "feat"), None), rows),
        check_vma=False,
    )
```

```python
import functools

import jax
import jax.numpy as jnp
from jax import lax
from jax.experimental import pallas as pl
from jax.experimental.pallas import tpu as pltpu
from jax.sharding import PartitionSpec as P

MESH = pl.DeviceIdType.MESH
LANES = 128
BF = jnp.bfloat16
F32 = jnp.float32


def dot(a, b):
    return jnp.dot(a, b, preferred_element_type=F32)


def normed(values, gain):
    mean = jnp.mean(values, axis=-1, keepdims=True)
    centred = values - mean
    spread = jnp.mean(centred * centred, axis=-1, keepdims=True)
    return centred * lax.rsqrt(spread + 1e-05) * gain


def silu(x):
    half = 0.5 * x
    return half + half * jnp.tanh(half)


def columns(row):
    return jnp.transpose(jnp.broadcast_to(row, (LANES, row.shape[1])))


def pick(cols, width):
    lane = lax.broadcasted_iota(jnp.int32, cols.shape, 1)
    if width < LANES:
        cols, lane = cols[:, :width], lane[:, :width]
        return jnp.where(cols == lane, 1.0, 0.0).astype(BF)
    parts = [
        jnp.where(cols == lane + t * LANES, 1.0, 0.0).astype(BF) for t in range(width // LANES)
    ]
    return parts[0] if len(parts) == 1 else jnp.concatenate(parts, axis=1)


NAMES = (
    "grid", "mesh", "g_send", "g_slot", "g_recv", "e_sw", "e_rw", "e_b", "e_ow", "e_g",
    "p_send", "p_slot", "p_recv", "p_sw", "p_rw", "p_b", "p_ow", "p_g",
    "m_send", "m_slot", "d_sw", "d_rw", "d_b", "d_ow", "d_g",
)
FIRST = ("g_send", "e_sw", "grid", "m_send")
SECOND = ("d_rw", "d_b", "mesh", "e_rw", "e_b", "m_slot", "g_slot", "g_recv", "e_ow", "e_g")
THIRD = ("p_send", "p_slot", "p_recv", "p_sw", "p_rw", "p_b", "p_ow", "p_g", "d_sw", "d_ow", "d_g")


def kernel(nb, nm, cap_g, cap_h, cap_m, *refs):
    count = len(NAMES)
    sources = dict(zip(NAMES, refs[:count]))
    grid_out, mesh_out = refs[count : count + 2]
    here = dict(zip(NAMES, refs[count + 2 : 2 * count + 2]))
    (
        gp, ebuf, erecv, ecol, hid, acc, hid2, gcol, own_term, pbuf, precv, mbuf, iref, dcol, dproj, dtab,
        part, other, ls,
        es, er, is_, ir, ps, pr, ds, dr, fs, fr, ws, wr,
    ) = refs[2 * count + 2 :]

    def fetch(name):
        return pltpu.make_async_copy(sources[name], here[name], ls.at[NAMES.index(name)])

    def ready(*names):
        for name in names:
            fetch(name).wait()

    for name in FIRST:
        fetch(name).start()

    def flat(name):
        value = here[name][...]
        return value.reshape(1, value.shape[0])

    grid_ref, mesh_ref = here["grid"], here["mesh"]
    e_sw, e_rw, e_ow = here["e_sw"], here["e_rw"], here["e_ow"]
    p_sw, p_rw, p_ow = here["p_sw"], here["p_rw"], here["p_ow"]
    d_sw, d_rw, d_ow = here["d_sw"], here["d_rw"], here["d_ow"]
    band, col, feat = lax.axis_index("band"), lax.axis_index("mesh"), lax.axis_index("feat")
    me = band * nm + col
    shards = nb * nm
    mrows = mesh_ref.shape[0]
    half = grid_out.shape[0]
    dh = e_sw.shape[1]
    near = 3 * nm

    def at_shard(shard):
        return {"band": shard // nm, "mesh": lax.rem(shard, nm)}

    barrier = pltpu.get_barrier_semaphore()
    for o in range(1, shards):
        peer = lax.rem(me + o, shards)
        pl.semaphore_signal(barrier, inc=1, device_id=at_shard(peer), device_id_type=MESH)
    pl.semaphore_signal(barrier, inc=1, device_id={"feat": 1 - feat}, device_id_type=MESH)

    for name in SECOND:
        fetch(name).start()
    ready("g_send", "e_sw", "grid", "m_send")
    gp[...] = dot(grid_ref[...], e_sw[...]).astype(BF)
    for d, edge in ((0, 0), (2, nb - 1)):
        @pl.when(band == edge)
        def _(d=d):
            for j in range(nm):
                i = d * nm + j
                erecv[i] = jnp.zeros(erecv.shape[1:], BF)
                iref[i] = jnp.zeros(iref.shape[1:], jnp.int32)
                for f in range(2):
                    dtab[f, i] = jnp.zeros(dtab.shape[2:], BF)

    pl.semaphore_wait(barrier, shards)

    def near_copy(src, dst, send, recv, d, o):
        to = lax.rem(col + o, nm)
        return pltpu.make_async_remote_copy(
            src_ref=src(d * nm + to),
            dst_ref=dst.at[d * nm + col],
            send_sem=send.at[d * nm + o],
            recv_sem=recv.at[d * nm + col],
            device_id={"band": band + 1 - d, "mesh": to},
            device_id_type=MESH,
        )

    def near_arrival(dst, send, recv, d, o):
        source = lax.rem(col + o, nm)
        return pltpu.make_async_remote_copy(
            src_ref=dst.at[d * nm + source],
            dst_ref=dst.at[d * nm + source],
            send_sem=send.at[d * nm + o],
            recv_sem=recv.at[d * nm + source],
            device_id={"band": band + d - 1, "mesh": source},
            device_id_type=MESH,
        )

    def to_there(d):
        return {0: band + 1 < nb, 2: band > 0, 1: None}[d]

    def from_there(d):
        return {0: band > 0, 2: band + 1 < nb, 1: None}[d]

    def when(cond, f):
        if cond is None:
            f()
        else:
            pl.when(cond)(f)

    across = [(d, o) for d in (0, 2, 1) for o in range(1, nm)]
    along = [(0, 0), (2, 0)]
    order = across + along

    for name in THIRD:
        fetch(name).start()

    for i in range(near):
        mbuf[i] = flat("m_send")[:, i * cap_m : (i + 1) * cap_m]
    for d, o in order:
        when(to_there(d), lambda d=d, o=o: near_copy(lambda i: mbuf.at[i], iref, is_, ir, d, o).start())
    iref[nm + col] = mbuf[nm + col]

    for i in range(near):
        gcol[i] = columns(flat("g_send")[:, i * cap_g : (i + 1) * cap_g])

    def gathered(i):
        return dot(pick(gcol[i], gp.shape[0]), gp[...]).astype(BF)

    for d, o in order:
        def send(d=d, o=o):
            i = d * nm + lax.rem(col + o, nm)
            ebuf[i] = gathered(i)
            near_copy(lambda i: ebuf.at[i], erecv, es, er, d, o).start()
        when(to_there(d), send)
    erecv[nm + col] = gathered(nm + col)

    ready(*SECOND)
    own = pl.ds(pl.multiple_of(feat * half, half), half)
    own_term[...] = dot(grid_ref[own, :], d_rw[...]) + flat("d_b")

    def split_term(values, weight, bias):
        term = dot(values, weight[...]) + bias
        high = term.astype(BF)
        return jnp.concatenate([high, (term - high.astype(F32)).astype(BF)], axis=0)

    def pick2(cols):
        lane = lax.broadcasted_iota(jnp.int32, cols.shape, 1)
        if 2 * mrows == LANES:
            lane = jnp.where(lane >= mrows, lane - mrows, lane)
            return jnp.where(cols == lane, 1.0, 0.0).astype(BF)
        single = pick(cols, mrows)
        return jnp.concatenate([single, single], axis=1)

    eterm = split_term(mesh_ref[...], e_rw, flat("e_b"))

    for d, o in order:
        when(from_there(d), lambda d=d, o=o: near_arrival(iref, is_, ir, d, o).wait_recv())
    tables = [columns(iref[i]).astype(F32).astype(BF) for i in range(near)]
    for k in range(3):
        slots = columns(flat("m_slot")[:, k * half : (k + 1) * half])
        block = jnp.zeros(slots.shape, jnp.int32)
        row = jnp.zeros(slots.shape, F32)
        for i in range(near):
            row = row + dot(pick(slots - i * cap_m, cap_m), tables[i])
            if i:
                block = block + jnp.where(slots >= i * cap_m, mrows, 0)
        dcol[pl.ds(k * half, half), :] = block + (row + 0.5).astype(jnp.int32)

    ecol[0] = columns(flat("g_slot"))
    ecol[1] = columns(flat("g_recv"))
    chunk = 256

    def block_terms(rows, blocks):
        cols = ecol[0, rows, :]
        hot = jnp.concatenate([pick(cols - i * cap_g, cap_g) for i in blocks], axis=1)
        return dot(hot, jnp.concatenate([erecv[i] for i in blocks], axis=0))

    def chunks(body):
        def step(c, carry):
            body(pl.ds(pl.multiple_of(c * chunk, chunk), chunk))
            return carry

        lax.fori_loop(0, hid.shape[0] // chunk, step, 0)

    def arrived(pairs):
        for d, o in pairs:
            when(from_there(d), lambda d=d, o=o: near_arrival(erecv, es, er, d, o).wait_recv())

    arrived(along)

    def early(rows):
        acc[rows, :] = block_terms(rows, [d * nm + col for d in range(3)]) + dot(
            pick2(ecol[1, rows, :]), eterm
        )

    def late(rows):
        blocks = [d * nm + lax.rem(col + o, nm) for d in range(3) for o in range(1, nm)]
        hid[rows, :] = silu(acc[rows, :] + block_terms(rows, blocks)).astype(BF)

    chunks(early)
    arrived(across)
    chunks(late)

    def finish(base, recv, hidden, ow, gain, n):
        place = lax.broadcasted_iota(jnp.int32, (mrows, recv.shape[1]), 0)
        onto = jnp.where(recv == place, 1.0, 0.0).astype(BF)
        summed = dot(onto, hidden[...]).astype(BF)
        part[n] = dot(summed, ow[...]).astype(BF)
        copy = pltpu.make_async_remote_copy(
            src_ref=part.at[n], dst_ref=other.at[n], send_sem=fs.at[n], recv_sem=fr.at[n],
            device_id={"feat": 1 - feat}, device_id_type=MESH,
        )
        copy.start()
        copy.wait()
        total = part[n].astype(F32) + other[n].astype(F32)
        return (base.astype(F32) + normed(total, gain)).astype(BF)

    ready(*THIRD)
    psend_pick = pick(columns(flat("p_send")), mrows)
    pslot_pick = pick(columns(flat("p_slot")), shards * cap_h)
    precv_pick = pick2(columns(flat("p_recv")))
    first = finish(mesh_ref[...], flat("g_recv"), hid, e_ow, flat("e_g"), 0)

    mproj = dot(first, p_sw[...]).astype(BF)
    pbuf[...] = dot(psend_pick, mproj).astype(BF).reshape(pbuf.shape)

    def proc_copy(o):
        peer = lax.rem(me + o, shards)
        return pltpu.make_async_remote_copy(
            src_ref=pbuf.at[peer], dst_ref=precv.at[me], send_sem=ps.at[o], recv_sem=pr.at[me],
            device_id=at_shard(peer), device_id_type=MESH,
        )

    def proc_arrival(o):
        peer = lax.rem(me + o, shards)
        return pltpu.make_async_remote_copy(
            src_ref=precv.at[peer], dst_ref=precv.at[peer], send_sem=ps.at[o],
            recv_sem=pr.at[peer], device_id=at_shard(peer), device_id_type=MESH,
        )

    for o in range(1, shards):
        proc_copy(o).start()
    precv[me] = pbuf[me]
    pterm = dot(precv_pick, split_term(first, p_rw, flat("p_b")))
    for o in range(1, shards):
        proc_arrival(o).wait_recv()
    pre = dot(pslot_pick, precv[...].reshape(shards * cap_h, dh)) + pterm
    hid2[...] = silu(pre).astype(BF)
    last = finish(first, flat("p_recv"), hid2, p_ow, flat("p_g"), 1)
    mesh_out[...] = last

    side = dproj.shape[1]
    projected = dot(last, d_sw[:, pl.ds(pl.multiple_of(feat * side, side), side)]).astype(BF)
    dproj[...] = projected
    for d, o in order:
        when(to_there(d), lambda d=d, o=o: near_copy(lambda i: dproj, dtab.at[feat], ds, dr, d, o).start())
    dtab[feat, nm + col] = projected

    def passed(i, half_of):
        return pltpu.make_async_remote_copy(
            src_ref=dtab.at[half_of, i], dst_ref=dtab.at[half_of, i],
            send_sem=ws.at[i], recv_sem=wr.at[i],
            device_id={"feat": 1 - feat}, device_id_type=MESH,
        )

    passed(nm + col, feat).start()
    hops = along + [(1, o) for o in range(1, nm)] + [p for p in across if p[0] != 1]

    def pass_on(d, o):
        near_arrival(dtab.at[feat], ds, dr, d, o).wait_recv()
        passed(d * nm + lax.rem(col + o, nm), feat).start()

    for d, o in hops:
        when(from_there(d), lambda d=d, o=o: pass_on(d, o))
    for d, o in [(1, 0)] + hops:
        when(from_there(d), lambda d=d, o=o: passed(
            d * nm + lax.rem(col + o, nm), 1 - feat).wait_recv())
    dchunk = 128

    def decode(c, carry):
        rows = pl.ds(pl.multiple_of(c * dchunk, dchunk), dchunk)
        term = own_term[rows, :]
        tables = [dtab[f].reshape(near * mrows, side) for f in range(2)]
        summed = jnp.zeros(term.shape, F32)
        for k in range(3):
            idx = dcol[pl.ds(3 * c * dchunk + k, dchunk, stride=3), :]
            hot = pick(idx, near * mrows)
            pre = jnp.concatenate([dot(hot, t) for t in tables], axis=1) + term
            summed = summed + silu(pre).astype(BF).astype(F32)
        decoded = dot(summed.astype(BF), d_ow[...])
        base = grid_ref[pl.ds(pl.multiple_of(feat * half + c * dchunk, dchunk), dchunk), :]
        grid_out[rows, :] = (base.astype(F32) + normed(decoded, flat("d_g"))).astype(BF)
        return carry

    lax.fori_loop(0, half // dchunk, decode, 0)

    for d, o in order:
        def done(d=d, o=o):
            near_copy(lambda i: mbuf.at[i], iref, is_, ir, d, o).wait_send()
            near_copy(lambda i: ebuf.at[i], erecv, es, er, d, o).wait_send()
            near_copy(lambda i: dproj, dtab.at[feat], ds, dr, d, o).wait_send()
        when(to_there(d), done)
    for d, o in [(1, 0)] + hops:
        when(from_there(d), lambda d=d, o=o: passed(
            d * nm + lax.rem(col + o, nm), feat).wait_send())
    for o in range(1, shards):
        proc_copy(o).wait_send()


def per_device(
    grid_latent, mesh_latent,
    g2m_send, g2m_slot, g2m_recv, enc_send_w, enc_recv_w, enc_bias, enc_out_w, enc_gain,
    proc_send, proc_slot, proc_recv, proc_send_w, proc_recv_w, proc_bias, proc_out_w, proc_gain,
    m2g_send, m2g_slot, dec_send_w, dec_recv_w, dec_bias, dec_out_w, dec_gain,
):
    nb, nm = lax.axis_size("band"), lax.axis_size("mesh")
    shards, near = nb * nm, 3 * nm
    rows, width = grid_latent.shape
    mrows = mesh_latent.shape[0]
    half = rows // lax.axis_size("feat")
    dh = enc_send_w.shape[1]
    cap_g = g2m_send.shape[0] // near
    cap_m = m2g_send.shape[0] // near
    cap_h = proc_send.shape[0] // shards
    if cap_h % 16:
        padded = -(-cap_h // 16) * 16
        proc_send = jnp.pad(proc_send.reshape(shards, cap_h), ((0, 0), (0, padded - cap_h))).reshape(-1)
        proc_slot = proc_slot // cap_h * padded + proc_slot % cap_h
        cap_h = padded
    args = (
        grid_latent, mesh_latent,
        g2m_send, g2m_slot, g2m_recv, enc_send_w, enc_recv_w, enc_bias, enc_out_w, enc_gain,
        proc_send, proc_slot, proc_recv,
        proc_send_w, proc_recv_w, proc_bias, proc_out_w, proc_gain,
        m2g_send, m2g_slot, dec_send_w, dec_recv_w, dec_bias, dec_out_w, dec_gain,
    )
    hbm = pl.BlockSpec(memory_space=pltpu.HBM)
    vmem = pl.BlockSpec(memory_space=pltpu.VMEM)
    dma = pltpu.SemaphoreType.DMA
    scratch = [pltpu.VMEM(v.shape, v.dtype) for v in args] + [
        pltpu.VMEM((rows, dh), BF),
        pltpu.VMEM((near, cap_g, dh), BF),
        pltpu.VMEM((near, cap_g, dh), BF),
        pltpu.VMEM((2, g2m_slot.shape[0], LANES), jnp.int32),
        pltpu.VMEM((g2m_slot.shape[0], dh), BF),
        pltpu.VMEM((g2m_slot.shape[0], dh), F32),
        pltpu.VMEM((proc_slot.shape[0], dh), BF),
        pltpu.VMEM((near, cap_g, LANES), jnp.int32),
        pltpu.VMEM((half, width), F32),
        pltpu.VMEM((shards, cap_h, dh), BF),
        pltpu.VMEM((shards, cap_h, dh), BF),
        pltpu.VMEM((near, 1, cap_m), jnp.int32),
        pltpu.VMEM((near, 1, cap_m), jnp.int32),
        pltpu.VMEM((3 * half, LANES), jnp.int32),
        pltpu.VMEM((mrows, width // 2), BF),
        pltpu.VMEM((2, near, mrows, width // 2), BF),
        pltpu.VMEM((2, mrows, width), BF),
        pltpu.VMEM((2, mrows, width), BF),
        dma((len(args),)),
        dma((near,)), dma((near,)), dma((near,)), dma((near,)),
        dma((shards,)), dma((shards,)), dma((near,)), dma((near,)),
        dma((2,)), dma((2,)), dma((near,)), dma((near,)),
    ]
    grid_out, mesh_out = pl.pallas_call(
        functools.partial(kernel, nb, nm, cap_g, cap_h, cap_m),
        out_shape=(
            jax.ShapeDtypeStruct((half, width), BF),
            jax.ShapeDtypeStruct((mrows, width), BF),
        ),
        in_specs=[hbm] * len(args),
        out_specs=(vmem, vmem),
        scratch_shapes=scratch,
        compiler_params=pltpu.CompilerParams(
            collective_id=0, has_side_effects=True, vmem_limit_bytes=64 * 1024 * 1024
        ),
    )(*args)
    return (grid_out, mesh_out)


def solution(mesh):
    shard = P(("groups", "band", "mesh"))
    rows = P(("groups", "band", "mesh"), None)
    finer = P(("groups", "band", "mesh", "feat"))
    layer = (P(None, "feat"), P(None, "feat"), P("feat"), P("feat", None), P())
    return jax.shard_map(
        per_device,
        mesh=mesh,
        in_specs=(rows, rows, shard, shard, shard, *layer, shard, shard, shard, *layer,
                  finer, finer, P(), P(), P(), P(), P()),
        out_specs=(P(("groups", "band", "mesh", "feat"), None), rows),
        check_vma=False,
    )
```

```python
import functools

import jax
import jax.numpy as jnp
from jax import lax
from jax.experimental import pallas as pl
from jax.experimental.pallas import tpu as pltpu
from jax.sharding import PartitionSpec as P

MESH = pl.DeviceIdType.MESH
LANES = 128
BF = jnp.bfloat16
F32 = jnp.float32


def dot(a, b):
    return jnp.dot(a, b, preferred_element_type=F32)


def normed(values, gain):
    mean = jnp.mean(values, axis=-1, keepdims=True)
    centred = values - mean
    spread = jnp.mean(centred * centred, axis=-1, keepdims=True)
    return centred * lax.rsqrt(spread + 1e-05) * gain


def silu(x):
    half = 0.5 * x
    return half + half * jnp.tanh(half)


def columns(row):
    return jnp.transpose(jnp.broadcast_to(row, (LANES, row.shape[1])))


def pick(cols, width):
    lane = lax.broadcasted_iota(jnp.int32, cols.shape, 1)
    if width < LANES:
        cols, lane = cols[:, :width], lane[:, :width]
        return jnp.where(cols == lane, 1.0, 0.0).astype(BF)
    parts = [
        jnp.where(cols == lane + t * LANES, 1.0, 0.0).astype(BF) for t in range(width // LANES)
    ]
    return parts[0] if len(parts) == 1 else jnp.concatenate(parts, axis=1)


NAMES = (
    "grid", "mesh", "g_send", "g_slot", "g_recv", "e_sw", "e_rw", "e_b", "e_ow", "e_g",
    "p_send", "p_slot", "p_recv", "p_sw", "p_rw", "p_b", "p_ow", "p_g",
    "m_send", "m_slot", "d_sw", "d_rw", "d_b", "d_ow", "d_g",
)
FIRST = ("g_send", "e_sw", "grid", "m_send")
SECOND = ("d_rw", "d_b", "mesh", "e_rw", "e_b", "m_slot", "g_slot", "g_recv", "e_ow", "e_g")
THIRD = ("p_send", "p_slot", "p_recv", "p_sw", "p_rw", "p_b", "p_ow", "p_g", "d_sw", "d_ow", "d_g")


def kernel(nb, nm, cap_g, cap_h, cap_m, *refs):
    count = len(NAMES)
    sources = dict(zip(NAMES, refs[:count]))
    grid_out, mesh_out = refs[count : count + 2]
    here = dict(zip(NAMES, refs[count + 2 : 2 * count + 2]))
    (
        gp, ebuf, erecv, ecol, hid, hid2, gcol, own_term, pbuf, precv, mbuf, iref, dcol, dproj, dtab,
        part, other, ls,
        es, er, is_, ir, ps, pr, ds, dr, fs, fr,
    ) = refs[2 * count + 2 :]

    def fetch(name):
        return pltpu.make_async_copy(sources[name], here[name], ls.at[NAMES.index(name)])

    def ready(*names):
        for name in names:
            fetch(name).wait()

    for name in FIRST:
        fetch(name).start()

    def flat(name):
        value = here[name][...]
        return value.reshape(1, value.shape[0])

    grid_ref, mesh_ref = here["grid"], here["mesh"]
    e_sw, e_rw, e_ow = here["e_sw"], here["e_rw"], here["e_ow"]
    p_sw, p_rw, p_ow = here["p_sw"], here["p_rw"], here["p_ow"]
    d_sw, d_rw, d_ow = here["d_sw"], here["d_rw"], here["d_ow"]
    band, col, feat = lax.axis_index("band"), lax.axis_index("mesh"), lax.axis_index("feat")
    me = band * nm + col
    shards = nb * nm
    mrows = mesh_ref.shape[0]
    half = grid_out.shape[0]
    dh = e_sw.shape[1]
    near = 3 * nm

    def at_shard(shard):
        return {"band": shard // nm, "mesh": lax.rem(shard, nm)}

    barrier = pltpu.get_barrier_semaphore()
    for o in range(1, shards):
        peer = lax.rem(me + o, shards)
        pl.semaphore_signal(barrier, inc=1, device_id=at_shard(peer), device_id_type=MESH)
    pl.semaphore_signal(barrier, inc=1, device_id={"feat": 1 - feat}, device_id_type=MESH)

    for name in SECOND:
        fetch(name).start()
    ready("g_send", "e_sw", "grid", "m_send")
    gp[...] = dot(grid_ref[...], e_sw[...]).astype(BF)
    for d, edge in ((0, 0), (2, nb - 1)):
        @pl.when(band == edge)
        def _(d=d):
            for j in range(nm):
                i = d * nm + j
                erecv[i] = jnp.zeros(erecv.shape[1:], BF)
                iref[i] = jnp.zeros(iref.shape[1:], jnp.int32)
                dtab[i] = jnp.zeros(dtab.shape[1:], BF)

    pl.semaphore_wait(barrier, shards)

    def near_copy(src, dst, send, recv, d, o):
        to = lax.rem(col + o, nm)
        return pltpu.make_async_remote_copy(
            src_ref=src(d * nm + to),
            dst_ref=dst.at[d * nm + col],
            send_sem=send.at[d * nm + o],
            recv_sem=recv.at[d * nm + col],
            device_id={"band": band + 1 - d, "mesh": to},
            device_id_type=MESH,
        )

    def near_arrival(dst, send, recv, d, o):
        source = lax.rem(col + o, nm)
        return pltpu.make_async_remote_copy(
            src_ref=dst.at[d * nm + source],
            dst_ref=dst.at[d * nm + source],
            send_sem=send.at[d * nm + o],
            recv_sem=recv.at[d * nm + source],
            device_id={"band": band + d - 1, "mesh": source},
            device_id_type=MESH,
        )

    def to_there(d):
        return {0: band + 1 < nb, 2: band > 0, 1: None}[d]

    def from_there(d):
        return {0: band > 0, 2: band + 1 < nb, 1: None}[d]

    def when(cond, f):
        if cond is None:
            f()
        else:
            pl.when(cond)(f)

    order = [(d, o) for d in (0, 2, 1) for o in range(1, nm)] + [(0, 0), (2, 0)]

    for name in THIRD:
        fetch(name).start()

    for i in range(near):
        mbuf[i] = flat("m_send")[:, i * cap_m : (i + 1) * cap_m]
    for d, o in order:
        when(to_there(d), lambda d=d, o=o: near_copy(lambda i: mbuf.at[i], iref, is_, ir, d, o).start())
    iref[nm + col] = mbuf[nm + col]

    for i in range(near):
        gcol[i] = columns(flat("g_send")[:, i * cap_g : (i + 1) * cap_g])

    def gathered(i):
        return dot(pick(gcol[i], gp.shape[0]), gp[...]).astype(BF)

    for d, o in order:
        def send(d=d, o=o):
            i = d * nm + lax.rem(col + o, nm)
            ebuf[i] = gathered(i)
            near_copy(lambda i: ebuf.at[i], erecv, es, er, d, o).start()
        when(to_there(d), send)
    erecv[nm + col] = gathered(nm + col)

    ready(*SECOND)
    own = pl.ds(pl.multiple_of(feat * half, half), half)
    own_term[...] = dot(grid_ref[own, :], d_rw[...]) + flat("d_b")

    def split_term(values, weight, bias):
        term = dot(values, weight[...]) + bias
        high = term.astype(BF)
        return jnp.concatenate([high, (term - high.astype(F32)).astype(BF)], axis=0)

    def pick2(cols):
        lane = lax.broadcasted_iota(jnp.int32, cols.shape, 1)
        if 2 * mrows == LANES:
            lane = jnp.where(lane >= mrows, lane - mrows, lane)
            return jnp.where(cols == lane, 1.0, 0.0).astype(BF)
        single = pick(cols, mrows)
        return jnp.concatenate([single, single], axis=1)

    eterm = split_term(mesh_ref[...], e_rw, flat("e_b"))

    for d, o in order:
        when(from_there(d), lambda d=d, o=o: near_arrival(iref, is_, ir, d, o).wait_recv())
    tables = [columns(iref[i]).astype(F32).astype(BF) for i in range(near)]
    for k in range(3):
        slots = columns(flat("m_slot")[:, k * half : (k + 1) * half])
        block = jnp.zeros(slots.shape, jnp.int32)
        row = jnp.zeros(slots.shape, F32)
        for i in range(near):
            row = row + dot(pick(slots - i * cap_m, cap_m), tables[i])
            if i:
                block = block + jnp.where(slots >= i * cap_m, mrows, 0)
        dcol[pl.ds(k * half, half), :] = block + (row + 0.5).astype(jnp.int32)

    ecol[0] = columns(flat("g_slot"))
    ecol[1] = columns(flat("g_recv"))
    for d, o in order:
        when(from_there(d), lambda d=d, o=o: near_arrival(erecv, es, er, d, o).wait_recv())
    chunk = 768

    def edges(c, carry):
        rows = pl.ds(pl.multiple_of(c * chunk, chunk), chunk)
        pre = dot(pick(ecol[0, rows, :], near * cap_g), erecv[...].reshape(near * cap_g, dh))
        pre = pre.astype(BF).astype(F32) + dot(pick2(ecol[1, rows, :]), eterm)
        hid[rows, :] = silu(pre).astype(BF)
        return carry

    lax.fori_loop(0, hid.shape[0] // chunk, edges, 0)

    def finish(base, recv, hidden, ow, gain, n):
        place = lax.broadcasted_iota(jnp.int32, (mrows, recv.shape[1]), 0)
        onto = jnp.where(recv == place, 1.0, 0.0).astype(BF)
        summed = dot(onto, hidden[...]).astype(BF)
        part[n] = dot(summed, ow[...]).astype(BF)
        copy = pltpu.make_async_remote_copy(
            src_ref=part.at[n], dst_ref=other.at[n], send_sem=fs.at[n], recv_sem=fr.at[n],
            device_id={"feat": 1 - feat}, device_id_type=MESH,
        )
        copy.start()
        copy.wait()
        total = part[n].astype(F32) + other[n].astype(F32)
        return (base.astype(F32) + normed(total, gain)).astype(BF)

    ready(*THIRD)
    psend_pick = pick(columns(flat("p_send")), mrows)
    pslot_pick = pick(columns(flat("p_slot")), shards * cap_h)
    precv_pick = pick2(columns(flat("p_recv")))
    first = finish(mesh_ref[...], flat("g_recv"), hid, e_ow, flat("e_g"), 0)

    mproj = dot(first, p_sw[...]).astype(BF)
    pbuf[...] = dot(psend_pick, mproj).astype(BF).reshape(pbuf.shape)

    def proc_copy(o):
        peer = lax.rem(me + o, shards)
        return pltpu.make_async_remote_copy(
            src_ref=pbuf.at[peer], dst_ref=precv.at[me], send_sem=ps.at[o], recv_sem=pr.at[me],
            device_id=at_shard(peer), device_id_type=MESH,
        )

    def proc_arrival(o):
        peer = lax.rem(me + o, shards)
        return pltpu.make_async_remote_copy(
            src_ref=precv.at[peer], dst_ref=precv.at[peer], send_sem=ps.at[o],
            recv_sem=pr.at[peer], device_id=at_shard(peer), device_id_type=MESH,
        )

    for o in range(1, shards):
        proc_copy(o).start()
    precv[me] = pbuf[me]
    pterm = dot(precv_pick, split_term(first, p_rw, flat("p_b")))
    for o in range(1, shards):
        proc_arrival(o).wait_recv()
    pre = dot(pslot_pick, precv[...].reshape(shards * cap_h, dh)) + pterm
    hid2[...] = silu(pre).astype(BF)
    last = finish(first, flat("p_recv"), hid2, p_ow, flat("p_g"), 1)
    mesh_out[...] = last

    projected = dot(last, d_sw[...]).astype(BF)
    dproj[...] = projected
    for d, o in order:
        when(to_there(d), lambda d=d, o=o: near_copy(lambda i: dproj, dtab, ds, dr, d, o).start())
    dtab[nm + col] = projected
    for d, o in order:
        when(from_there(d), lambda d=d, o=o: near_arrival(dtab, ds, dr, d, o).wait_recv())
    dchunk = 512

    def decode(c, carry):
        rows = pl.ds(pl.multiple_of(c * dchunk, dchunk), dchunk)
        term = own_term[rows, :]
        table = dtab[...].reshape(near * mrows, dtab.shape[2])
        summed = jnp.zeros(term.shape, F32)
        for k in range(3):
            idx = dcol[pl.ds(3 * c * dchunk + k, dchunk, stride=3), :]
            pre = dot(pick(idx, near * mrows), table) + term
            summed = summed + silu(pre).astype(BF).astype(F32)
        decoded = dot(summed.astype(BF), d_ow[...])
        base = grid_ref[pl.ds(pl.multiple_of(feat * half + c * dchunk, dchunk), dchunk), :]
        grid_out[rows, :] = (base.astype(F32) + normed(decoded, flat("d_g"))).astype(BF)
        return carry

    lax.fori_loop(0, half // dchunk, decode, 0)

    for d, o in order:
        def done(d=d, o=o):
            near_copy(lambda i: mbuf.at[i], iref, is_, ir, d, o).wait_send()
            near_copy(lambda i: ebuf.at[i], erecv, es, er, d, o).wait_send()
            near_copy(lambda i: dproj, dtab, ds, dr, d, o).wait_send()
        when(to_there(d), done)
    for o in range(1, shards):
        proc_copy(o).wait_send()


def per_device(
    grid_latent, mesh_latent,
    g2m_send, g2m_slot, g2m_recv, enc_send_w, enc_recv_w, enc_bias, enc_out_w, enc_gain,
    proc_send, proc_slot, proc_recv, proc_send_w, proc_recv_w, proc_bias, proc_out_w, proc_gain,
    m2g_send, m2g_slot, dec_send_w, dec_recv_w, dec_bias, dec_out_w, dec_gain,
):
    nb, nm = lax.axis_size("band"), lax.axis_size("mesh")
    shards, near = nb * nm, 3 * nm
    rows, width = grid_latent.shape
    mrows = mesh_latent.shape[0]
    half = rows // lax.axis_size("feat")
    dh = enc_send_w.shape[1]
    cap_g = g2m_send.shape[0] // near
    cap_m = m2g_send.shape[0] // near
    cap_h = proc_send.shape[0] // shards
    if cap_h % 16:
        padded = -(-cap_h // 16) * 16
        proc_send = jnp.pad(proc_send.reshape(shards, cap_h), ((0, 0), (0, padded - cap_h))).reshape(-1)
        proc_slot = proc_slot // cap_h * padded + proc_slot % cap_h
        cap_h = padded
    args = (
        grid_latent, mesh_latent,
        g2m_send, g2m_slot, g2m_recv, enc_send_w, enc_recv_w, enc_bias, enc_out_w, enc_gain,
        proc_send, proc_slot, proc_recv,
        proc_send_w, proc_recv_w, proc_bias, proc_out_w, proc_gain,
        m2g_send, m2g_slot, dec_send_w, dec_recv_w, dec_bias, dec_out_w, dec_gain,
    )
    hbm = pl.BlockSpec(memory_space=pltpu.HBM)
    vmem = pl.BlockSpec(memory_space=pltpu.VMEM)
    dma = pltpu.SemaphoreType.DMA
    scratch = [pltpu.VMEM(v.shape, v.dtype) for v in args] + [
        pltpu.VMEM((rows, dh), BF),
        pltpu.VMEM((near, cap_g, dh), BF),
        pltpu.VMEM((near, cap_g, dh), BF),
        pltpu.VMEM((2, g2m_slot.shape[0], LANES), jnp.int32),
        pltpu.VMEM((g2m_slot.shape[0], dh), BF),
        pltpu.VMEM((proc_slot.shape[0], dh), BF),
        pltpu.VMEM((near, cap_g, LANES), jnp.int32),
        pltpu.VMEM((half, width), F32),
        pltpu.VMEM((shards, cap_h, dh), BF),
        pltpu.VMEM((shards, cap_h, dh), BF),
        pltpu.VMEM((near, 1, cap_m), jnp.int32),
        pltpu.VMEM((near, 1, cap_m), jnp.int32),
        pltpu.VMEM((3 * half, LANES), jnp.int32),
        pltpu.VMEM((mrows, width), BF),
        pltpu.VMEM((near, mrows, width), BF),
        pltpu.VMEM((2, mrows, width), BF),
        pltpu.VMEM((2, mrows, width), BF),
        dma((len(args),)),
        dma((near,)), dma((near,)), dma((near,)), dma((near,)),
        dma((shards,)), dma((shards,)), dma((near,)), dma((near,)),
        dma((2,)), dma((2,)),
    ]
    grid_out, mesh_out = pl.pallas_call(
        functools.partial(kernel, nb, nm, cap_g, cap_h, cap_m),
        out_shape=(
            jax.ShapeDtypeStruct((half, width), BF),
            jax.ShapeDtypeStruct((mrows, width), BF),
        ),
        in_specs=[hbm] * len(args),
        out_specs=(vmem, vmem),
        scratch_shapes=scratch,
        compiler_params=pltpu.CompilerParams(
            collective_id=0, has_side_effects=True, vmem_limit_bytes=64 * 1024 * 1024
        ),
    )(*args)
    return (grid_out, mesh_out)


def solution(mesh):
    shard = P(("groups", "band", "mesh"))
    rows = P(("groups", "band", "mesh"), None)
    finer = P(("groups", "band", "mesh", "feat"))
    layer = (P(None, "feat"), P(None, "feat"), P("feat"), P("feat", None), P())
    return jax.shard_map(
        per_device,
        mesh=mesh,
        in_specs=(rows, rows, shard, shard, shard, *layer, shard, shard, shard, *layer,
                  finer, finer, P(), P(), P(), P(), P()),
        out_specs=(P(("groups", "band", "mesh", "feat"), None), rows),
        check_vma=False,
    )
```

```python
import functools

import jax
import jax.numpy as jnp
from jax import lax
from jax.experimental import pallas as pl
from jax.experimental.pallas import tpu as pltpu
from jax.sharding import PartitionSpec as P

MESH = pl.DeviceIdType.MESH
LANES = 128
BF = jnp.bfloat16
F32 = jnp.float32


def dot(a, b):
    return jnp.dot(a, b, preferred_element_type=F32)


def normed(values, gain):
    mean = jnp.mean(values, axis=-1, keepdims=True)
    centred = values - mean
    spread = jnp.mean(centred * centred, axis=-1, keepdims=True)
    return centred * lax.rsqrt(spread + 1e-05) * gain


def silu(x):
    half = 0.5 * x
    return half + half * jnp.tanh(half)


def columns(row):
    return jnp.transpose(jnp.broadcast_to(row, (LANES, row.shape[1])))


def pick(cols, width):
    lane = lax.broadcasted_iota(jnp.int32, cols.shape, 1)
    if width < LANES:
        cols, lane = cols[:, :width], lane[:, :width]
        return jnp.where(cols == lane, 1.0, 0.0).astype(BF)
    parts = [
        jnp.where(cols == lane + t * LANES, 1.0, 0.0).astype(BF) for t in range(width // LANES)
    ]
    return parts[0] if len(parts) == 1 else jnp.concatenate(parts, axis=1)


NAMES = (
    "grid", "mesh", "g_send", "g_slot", "g_recv", "e_sw", "e_rw", "e_b", "e_ow", "e_g",
    "p_send", "p_slot", "p_recv", "p_sw", "p_rw", "p_b", "p_ow", "p_g",
    "m_send", "m_slot", "d_sw", "d_rw", "d_b", "d_ow", "d_g",
)
FIRST = ("g_send", "e_sw", "grid", "m_send")
SECOND = ("d_rw", "d_b", "mesh", "e_rw", "e_b", "m_slot", "g_slot", "g_recv", "e_ow", "e_g")
THIRD = ("p_send", "p_slot", "p_recv", "p_sw", "p_rw", "p_b", "p_ow", "p_g", "d_sw", "d_ow", "d_g")


def kernel(nb, nm, cap_g, cap_h, cap_m, *refs):
    count = len(NAMES)
    sources = dict(zip(NAMES, refs[:count]))
    grid_out, mesh_out = refs[count : count + 2]
    here = dict(zip(NAMES, refs[count + 2 : 2 * count + 2]))
    (
        gp, ebuf, erecv, ecol, hid, hid2, gcol, own_term, pbuf, precv, mbuf, iref, dcol, dproj, dtab,
        part, other, ls,
        es, er, is_, ir, ps, pr, ds, dr, fs, fr,
    ) = refs[2 * count + 2 :]

    def fetch(name):
        return pltpu.make_async_copy(sources[name], here[name], ls.at[NAMES.index(name)])

    def ready(*names):
        for name in names:
            fetch(name).wait()

    for name in FIRST:
        fetch(name).start()

    def flat(name):
        value = here[name][...]
        return value.reshape(1, value.shape[0])

    grid_ref, mesh_ref = here["grid"], here["mesh"]
    e_sw, e_rw, e_ow = here["e_sw"], here["e_rw"], here["e_ow"]
    p_sw, p_rw, p_ow = here["p_sw"], here["p_rw"], here["p_ow"]
    d_sw, d_rw, d_ow = here["d_sw"], here["d_rw"], here["d_ow"]
    band, col, feat = lax.axis_index("band"), lax.axis_index("mesh"), lax.axis_index("feat")
    me = band * nm + col
    shards = nb * nm
    mrows = mesh_ref.shape[0]
    half = grid_out.shape[0]
    dh = e_sw.shape[1]
    near = 3 * nm

    def at_shard(shard):
        return {"band": shard // nm, "mesh": lax.rem(shard, nm)}

    barrier = pltpu.get_barrier_semaphore()
    for o in range(1, shards):
        peer = lax.rem(me + o, shards)
        pl.semaphore_signal(barrier, inc=1, device_id=at_shard(peer), device_id_type=MESH)
    pl.semaphore_signal(barrier, inc=1, device_id={"feat": 1 - feat}, device_id_type=MESH)

    for name in SECOND:
        fetch(name).start()
    ready("g_send", "e_sw", "grid", "m_send")
    gp[...] = dot(grid_ref[...], e_sw[...]).astype(BF)
    for d, edge in ((0, 0), (2, nb - 1)):
        @pl.when(band == edge)
        def _(d=d):
            for j in range(nm):
                i = d * nm + j
                erecv[i] = jnp.zeros(erecv.shape[1:], BF)
                iref[i] = jnp.zeros(iref.shape[1:], jnp.int32)
                dtab[i] = jnp.zeros(dtab.shape[1:], BF)

    pl.semaphore_wait(barrier, shards)

    def near_copy(src, dst, send, recv, d, o):
        to = lax.rem(col + o, nm)
        return pltpu.make_async_remote_copy(
            src_ref=src(d * nm + to),
            dst_ref=dst.at[d * nm + col],
            send_sem=send.at[d * nm + o],
            recv_sem=recv.at[d * nm + col],
            device_id={"band": band + 1 - d, "mesh": to},
            device_id_type=MESH,
        )

    def near_arrival(dst, send, recv, d, o):
        source = lax.rem(col + o, nm)
        return pltpu.make_async_remote_copy(
            src_ref=dst.at[d * nm + source],
            dst_ref=dst.at[d * nm + source],
            send_sem=send.at[d * nm + o],
            recv_sem=recv.at[d * nm + source],
            device_id={"band": band + d - 1, "mesh": source},
            device_id_type=MESH,
        )

    def to_there(d):
        return {0: band + 1 < nb, 2: band > 0, 1: None}[d]

    def from_there(d):
        return {0: band > 0, 2: band + 1 < nb, 1: None}[d]

    def when(cond, f):
        if cond is None:
            f()
        else:
            pl.when(cond)(f)

    order = [(d, o) for d in (0, 2, 1) for o in range(1, nm)] + [(0, 0), (2, 0)]

    for name in THIRD:
        fetch(name).start()

    for i in range(near):
        mbuf[i] = flat("m_send")[:, i * cap_m : (i + 1) * cap_m]
    for d, o in order:
        when(to_there(d), lambda d=d, o=o: near_copy(lambda i: mbuf.at[i], iref, is_, ir, d, o).start())
    iref[nm + col] = mbuf[nm + col]

    for i in range(near):
        gcol[i] = columns(flat("g_send")[:, i * cap_g : (i + 1) * cap_g])

    def gathered(i):
        return dot(pick(gcol[i], gp.shape[0]), gp[...]).astype(BF)

    for d, o in order:
        def send(d=d, o=o):
            i = d * nm + lax.rem(col + o, nm)
            ebuf[i] = gathered(i)
            near_copy(lambda i: ebuf.at[i], erecv, es, er, d, o).start()
        when(to_there(d), send)
    erecv[nm + col] = gathered(nm + col)

    ready(*SECOND)
    own = pl.ds(pl.multiple_of(feat * half, half), half)
    own_term[...] = dot(grid_ref[own, :], d_rw[...]) + flat("d_b")

    def split_term(values, weight, bias):
        term = dot(values, weight[...]) + bias
        high = term.astype(BF)
        return jnp.concatenate([high, (term - high.astype(F32)).astype(BF)], axis=0)

    def pick2(cols):
        lane = lax.broadcasted_iota(jnp.int32, cols.shape, 1)
        if 2 * mrows == LANES:
            lane = jnp.where(lane >= mrows, lane - mrows, lane)
            return jnp.where(cols == lane, 1.0, 0.0).astype(BF)
        single = pick(cols, mrows)
        return jnp.concatenate([single, single], axis=1)

    eterm = split_term(mesh_ref[...], e_rw, flat("e_b"))

    for d, o in order:
        when(from_there(d), lambda d=d, o=o: near_arrival(iref, is_, ir, d, o).wait_recv())
    tables = [columns(iref[i]).astype(F32).astype(BF) for i in range(near)]
    for k in range(3):
        slots = columns(flat("m_slot")[:, k * half : (k + 1) * half])
        block = jnp.zeros(slots.shape, jnp.int32)
        row = jnp.zeros(slots.shape, F32)
        for i in range(near):
            row = row + dot(pick(slots - i * cap_m, cap_m), tables[i])
            if i:
                block = block + jnp.where(slots >= i * cap_m, mrows, 0)
        dcol[pl.ds(k * half, half), :] = block + (row + 0.5).astype(jnp.int32)

    ecol[0] = columns(flat("g_slot"))
    ecol[1] = columns(flat("g_recv"))
    ready(*THIRD)
    psend_pick = pick(columns(flat("p_send")), mrows)
    pslot_pick = pick(columns(flat("p_slot")), shards * cap_h)
    precv_pick = pick2(columns(flat("p_recv")))
    def onto(recv):
        place = lax.broadcasted_iota(jnp.int32, (mrows, recv.shape[1]), 0)
        return jnp.where(recv == place, 1.0, 0.0).astype(BF)

    g_onto, p_onto = onto(flat("g_recv")), onto(flat("p_recv"))
    for d, o in order:
        when(from_there(d), lambda d=d, o=o: near_arrival(erecv, es, er, d, o).wait_recv())
    chunk = 768

    def edges(c, carry):
        rows = pl.ds(pl.multiple_of(c * chunk, chunk), chunk)
        pre = dot(pick(ecol[0, rows, :], near * cap_g), erecv[...].reshape(near * cap_g, dh))
        pre = pre.astype(BF).astype(F32) + dot(pick2(ecol[1, rows, :]), eterm)
        hid[rows, :] = silu(pre).astype(BF)
        return carry

    lax.fori_loop(0, hid.shape[0] // chunk, edges, 0)

    def finish(base, recv, hidden, ow, gain, n):
        summed = dot(recv, hidden[...]).astype(BF)
        part[n] = dot(summed, ow[...]).astype(BF)
        copy = pltpu.make_async_remote_copy(
            src_ref=part.at[n], dst_ref=other.at[n], send_sem=fs.at[n], recv_sem=fr.at[n],
            device_id={"feat": 1 - feat}, device_id_type=MESH,
        )
        copy.start()
        copy.wait()
        total = part[n].astype(F32) + other[n].astype(F32)
        return (base.astype(F32) + normed(total, gain)).astype(BF)

    first = finish(mesh_ref[...], g_onto, hid, e_ow, flat("e_g"), 0)

    mproj = dot(first, p_sw[...]).astype(BF)
    pbuf[...] = dot(psend_pick, mproj).astype(BF).reshape(pbuf.shape)

    def proc_copy(o):
        peer = lax.rem(me + o, shards)
        return pltpu.make_async_remote_copy(
            src_ref=pbuf.at[peer], dst_ref=precv.at[me], send_sem=ps.at[o], recv_sem=pr.at[me],
            device_id=at_shard(peer), device_id_type=MESH,
        )

    def proc_arrival(o):
        peer = lax.rem(me + o, shards)
        return pltpu.make_async_remote_copy(
            src_ref=precv.at[peer], dst_ref=precv.at[peer], send_sem=ps.at[o],
            recv_sem=pr.at[peer], device_id=at_shard(peer), device_id_type=MESH,
        )

    for o in range(1, shards):
        proc_copy(o).start()
    precv[me] = pbuf[me]
    pterm = dot(precv_pick, split_term(first, p_rw, flat("p_b")))
    for o in range(1, shards):
        proc_arrival(o).wait_recv()
    pre = dot(pslot_pick, precv[...].reshape(shards * cap_h, dh)) + pterm
    hid2[...] = silu(pre).astype(BF)
    last = finish(first, p_onto, hid2, p_ow, flat("p_g"), 1)
    mesh_out[...] = last

    projected = dot(last, d_sw[...]).astype(BF)
    dproj[...] = projected
    for d, o in order:
        when(to_there(d), lambda d=d, o=o: near_copy(lambda i: dproj, dtab, ds, dr, d, o).start())
    dtab[nm + col] = projected
    for d, o in order:
        when(from_there(d), lambda d=d, o=o: near_arrival(dtab, ds, dr, d, o).wait_recv())
    dchunk = 512

    def decode(c, carry):
        rows = pl.ds(pl.multiple_of(c * dchunk, dchunk), dchunk)
        term = own_term[rows, :]
        table = dtab[...].reshape(near * mrows, dtab.shape[2])
        summed = jnp.zeros(term.shape, F32)
        for k in range(3):
            idx = dcol[pl.ds(3 * c * dchunk + k, dchunk, stride=3), :]
            pre = dot(pick(idx, near * mrows), table) + term
            summed = summed + silu(pre).astype(BF).astype(F32)
        decoded = dot(summed.astype(BF), d_ow[...])
        base = grid_ref[pl.ds(pl.multiple_of(feat * half + c * dchunk, dchunk), dchunk), :]
        grid_out[rows, :] = (base.astype(F32) + normed(decoded, flat("d_g"))).astype(BF)
        return carry

    lax.fori_loop(0, half // dchunk, decode, 0)

    for d, o in order:
        def done(d=d, o=o):
            near_copy(lambda i: mbuf.at[i], iref, is_, ir, d, o).wait_send()
            near_copy(lambda i: ebuf.at[i], erecv, es, er, d, o).wait_send()
            near_copy(lambda i: dproj, dtab, ds, dr, d, o).wait_send()
        when(to_there(d), done)
    for o in range(1, shards):
        proc_copy(o).wait_send()


def per_device(
    grid_latent, mesh_latent,
    g2m_send, g2m_slot, g2m_recv, enc_send_w, enc_recv_w, enc_bias, enc_out_w, enc_gain,
    proc_send, proc_slot, proc_recv, proc_send_w, proc_recv_w, proc_bias, proc_out_w, proc_gain,
    m2g_send, m2g_slot, dec_send_w, dec_recv_w, dec_bias, dec_out_w, dec_gain,
):
    nb, nm = lax.axis_size("band"), lax.axis_size("mesh")
    shards, near = nb * nm, 3 * nm
    rows, width = grid_latent.shape
    mrows = mesh_latent.shape[0]
    half = rows // lax.axis_size("feat")
    dh = enc_send_w.shape[1]
    cap_g = g2m_send.shape[0] // near
    cap_m = m2g_send.shape[0] // near
    cap_h = proc_send.shape[0] // shards
    if cap_h % 16:
        padded = -(-cap_h // 16) * 16
        proc_send = jnp.pad(proc_send.reshape(shards, cap_h), ((0, 0), (0, padded - cap_h))).reshape(-1)
        proc_slot = proc_slot // cap_h * padded + proc_slot % cap_h
        cap_h = padded
    args = (
        grid_latent, mesh_latent,
        g2m_send, g2m_slot, g2m_recv, enc_send_w, enc_recv_w, enc_bias, enc_out_w, enc_gain,
        proc_send, proc_slot, proc_recv,
        proc_send_w, proc_recv_w, proc_bias, proc_out_w, proc_gain,
        m2g_send, m2g_slot, dec_send_w, dec_recv_w, dec_bias, dec_out_w, dec_gain,
    )
    hbm = pl.BlockSpec(memory_space=pltpu.HBM)
    vmem = pl.BlockSpec(memory_space=pltpu.VMEM)
    dma = pltpu.SemaphoreType.DMA
    scratch = [pltpu.VMEM(v.shape, v.dtype) for v in args] + [
        pltpu.VMEM((rows, dh), BF),
        pltpu.VMEM((near, cap_g, dh), BF),
        pltpu.VMEM((near, cap_g, dh), BF),
        pltpu.VMEM((2, g2m_slot.shape[0], LANES), jnp.int32),
        pltpu.VMEM((g2m_slot.shape[0], dh), BF),
        pltpu.VMEM((proc_slot.shape[0], dh), BF),
        pltpu.VMEM((near, cap_g, LANES), jnp.int32),
        pltpu.VMEM((half, width), F32),
        pltpu.VMEM((shards, cap_h, dh), BF),
        pltpu.VMEM((shards, cap_h, dh), BF),
        pltpu.VMEM((near, 1, cap_m), jnp.int32),
        pltpu.VMEM((near, 1, cap_m), jnp.int32),
        pltpu.VMEM((3 * half, LANES), jnp.int32),
        pltpu.VMEM((mrows, width), BF),
        pltpu.VMEM((near, mrows, width), BF),
        pltpu.VMEM((2, mrows, width), BF),
        pltpu.VMEM((2, mrows, width), BF),
        dma((len(args),)),
        dma((near,)), dma((near,)), dma((near,)), dma((near,)),
        dma((shards,)), dma((shards,)), dma((near,)), dma((near,)),
        dma((2,)), dma((2,)),
    ]
    grid_out, mesh_out = pl.pallas_call(
        functools.partial(kernel, nb, nm, cap_g, cap_h, cap_m),
        out_shape=(
            jax.ShapeDtypeStruct((half, width), BF),
            jax.ShapeDtypeStruct((mrows, width), BF),
        ),
        in_specs=[hbm] * len(args),
        out_specs=(vmem, vmem),
        scratch_shapes=scratch,
        compiler_params=pltpu.CompilerParams(
            collective_id=0, has_side_effects=True, vmem_limit_bytes=64 * 1024 * 1024
        ),
    )(*args)
    return (grid_out, mesh_out)


def solution(mesh):
    shard = P(("groups", "band", "mesh"))
    rows = P(("groups", "band", "mesh"), None)
    finer = P(("groups", "band", "mesh", "feat"))
    layer = (P(None, "feat"), P(None, "feat"), P("feat"), P("feat", None), P())
    return jax.shard_map(
        per_device,
        mesh=mesh,
        in_specs=(rows, rows, shard, shard, shard, *layer, shard, shard, shard, *layer,
                  finer, finer, P(), P(), P(), P(), P()),
        out_specs=(P(("groups", "band", "mesh", "feat"), None), rows),
        check_vma=False,
    )
```
